128 devices in a mesh: lon: 16 (over x, y), lat: 8 (over z, core).
Axes of the slice: x: 4, y: 4, z: 4, core: 2. Of those that a mesh axis runs over, the one named last changes fastest.
Arguments:
- moments: float32 [128, 3, 128, 2048], P(None, None, 'lat', 'lon'), may hold values from -6 to 6
- observed: float32 [8, 16, 128, 1024], P('lat', 'lon'), may hold values from -6 to 6
- counts: int32 [8, 16], P('lat', 'lon'), may hold values from 341 to 1024, as said below
- near_kernel: bfloat16 [8, 16, 6144, 1024], P('lat', 'lon'), may hold values from -0.078125 to 0.078125
- dipole_basis: bfloat16 [8, 16, 6144, 64], P('lat', 'lon'), may hold values from -0.078125 to 0.078125
- reading_basis: bfloat16 [8, 16, 1024, 64], P('lat', 'lon'), may hold values from -0.75 to 0.75
- coupling: float32 [8, 16, 64, 8192], P('lat', 'lon'), may hold values from -0.0625 to 0.0625
- ranks: int32 [8, 16, 128], P('lat', 'lon'), may hold values from 0 to 64, as said below
Outputs:
- new_moments: float32 [128, 3, 128, 2048], P(None, None, 'lat', 'lon')
- misfit: float32 [8, 16, 128, 1024], P('lat', 'lon')
The draws below stay inside these ranges and needn't reach their ends.
Inputs may be any that keep to these rules, and one draw needn't show every extreme that they name: `counts`: the first and last latitude bands hold 1024 readings in every longitude band; the others hold 341 to 1024. `ranks`: entry j of a block is 0 exactly when j is that block itself (j = c * 8 + b), otherwise 64//4 to 64.
All inputs are finite; a program needn't handle non-finite values.
Results may differ from the reference program's by a relative error of at most 0.0025.
Values sent between devices are 32-bit elements; how exact they have to be, the bound alone decides.
A program may use at most 128 MiB of HBM per device.

```python
import jax
import jax.numpy as jnp
from jax import lax

MEMB = 128
CLAT = 16
CLON = 128
RDEV = 1024
RANK = 64
NDEV = 128
NLAT = 128
NLON = 2048
ND = 6144
N_LON = 16
N_LAT = 8


def draw_counts(key, part):
    key = jax.random.fold_in(key, 11)
    band_count = NLAT // CLAT
    column_count = NLON // CLON
    drawn_counts = jax.random.randint(key, (band_count, column_count), RDEV // 3, RDEV + 1)
    band_index = jnp.arange(band_count)[:, None]
    polar_band = (band_index == 0) | (band_index == band_count - 1)
    return jnp.where(polar_band, RDEV, drawn_counts).astype(jnp.int32)


def draw_ranks(key, part):
    key = jax.random.fold_in(key, 23)
    band_count = NLAT // CLAT
    column_count = NLON // CLON
    device_count = band_count * column_count
    drawn_ranks = jax.random.randint(key, (band_count, column_count, device_count), RANK // 4, RANK + 1)
    own_index = jnp.arange(column_count)[None, :] * band_count + jnp.arange(band_count)[:, None]
    target = jnp.arange(device_count)[None, None, :]
    drawn_ranks = jnp.where(target == own_index[:, :, None], 0, drawn_ranks)
    drawn_ranks = drawn_ranks.at[0, 0, 1].set(RANK)
    return drawn_ranks.astype(jnp.int32)


def block_levels(key, dims, split, low, largest):
    gain, own = 1.0, jax.random.fold_in(key, 6)
    for dim, shards_of in split:
        draws = jnp.exp(jax.random.uniform(jax.random.fold_in(own, dim), (shards_of,), jnp.float32, low / len(split), largest / len(split)))
        gain = gain * jnp.repeat(draws, dims[dim] // shards_of).reshape([-1 if axis == dim else 1 for axis in range(len(dims))])
    return gain


def normal_values(key, shape, scale, bound, shards=(), held_as=jnp.bfloat16):
    gain = block_levels(key, shape, shards, -0.22, 0.18) if shards else 1.0
    entries = jax.random.normal(key, shape, jnp.float32) * scale * gain
    return jnp.minimum(jnp.maximum(entries, -bound), bound).astype(held_as)


def setup_inputs(seed: int = 0) -> dict:
    keys = jax.random.split(jax.random.key(seed), 9)
    moments = normal_values(keys[0], (MEMB, 3, NLAT, NLON), 1.0, 6.0, ((2, 8), (3, 16)), jnp.float32)
    observed = normal_values(keys[1], (N_LAT, N_LON, MEMB, RDEV), 1.0, 6.0, ((0, 8), (1, 16)), jnp.float32)
    counts = draw_counts(jax.random.fold_in(keys[8], 71), 0)
    near_kernel = normal_values(keys[3], (N_LAT, N_LON, ND, RDEV), ND ** -0.5, 0.078125, ((0, 8), (1, 16)))
    dipole_basis = normal_values(keys[4], (N_LAT, N_LON, ND, RANK), ND ** -0.5, 0.078125, ((0, 8), (1, 16)))
    reading_basis = normal_values(keys[5], (N_LAT, N_LON, RDEV, RANK), RANK ** -0.5, 0.75, ((0, 8), (1, 16)))
    coupling = normal_values(keys[6], (N_LAT, N_LON, RANK, NDEV * RANK), (NDEV * RANK) ** -0.5, 0.0625, ((0, 8), (1, 16)), jnp.float32)
    ranks = draw_ranks(jax.random.fold_in(keys[8], 71), 0)
    return {"moments": moments, "observed": observed, "counts": counts, "near_kernel": near_kernel, "dipole_basis": dipole_basis, "reading_basis": reading_basis, "coupling": coupling, "ranks": ranks}


step_size = 0.5
lat_limit = 1.25
highest = lax.Precision.HIGHEST


def rank_mask(block_ranks):
    repeated = jnp.repeat(block_ranks, RANK)
    inner = jnp.tile(jnp.arange(RANK, dtype=jnp.int32), block_ranks.shape[0])
    column_ok = inner < repeated
    row_ok = jnp.arange(RANK, dtype=jnp.int32)[:, None] < repeated[None, :]
    return (row_ok & column_ok[None, :]).astype(jnp.float32)


def lon_major(stacked):
    return jnp.swapaxes(stacked, 0, 1).reshape((NDEV,) + stacked.shape[2:])


def smooth_field(field):
    row_index = jnp.arange(NLAT).astype(jnp.float32)
    spacing = 2.0 * lat_limit / NLAT
    latitude = -lat_limit + (row_index + 0.5) * spacing
    centre = jnp.cos(latitude)
    c_lon = (0.25 / (centre * centre))[:, None]
    c_north = (0.25 * jnp.cos(latitude + 0.5 * spacing) / centre)[:, None]
    c_south = (0.25 * jnp.cos(latitude - 0.5 * spacing) / centre)[:, None]
    zero_row = jnp.zeros_like(field[:, :, :1, :])
    north = jnp.concatenate([field[:, :, 1:, :], zero_row], axis=2)
    south = jnp.concatenate([zero_row, field[:, :, :-1, :]], axis=2)
    east = jnp.roll(field, -1, axis=3)
    west = jnp.roll(field, 1, axis=3)
    total = field + c_north * north + c_south * south + c_lon * (east + west)
    return total / (1.0 + c_north + c_south + 2.0 * c_lon)


def sketch_one(items):
    basis, block = items
    return lax.dot_general(basis, block, (((0,), (1,)), ((), ())), preferred_element_type=jnp.float32)


def far_one(items):
    owner, basis = items
    return lax.dot_general(owner, basis, (((0,), (1,)), ((), ())), preferred_element_type=jnp.float32)


def reference(moments, observed, counts, near_kernel, dipole_basis, reading_basis, coupling, ranks):
    mbits = moments.astype(jnp.bfloat16)
    blocks = mbits.reshape(MEMB, 3, N_LAT, CLAT, N_LON, CLON).transpose(4, 2, 0, 1, 3, 5).reshape(NDEV, MEMB, ND)
    near_all = lon_major(near_kernel)
    dipole_all = lon_major(dipole_basis)
    reading_all = lon_major(reading_basis)
    coupling_all = lon_major(coupling)
    ranks_all = lon_major(ranks)
    observed_all = lon_major(observed)
    counts_all = lon_major(counts)
    sketches = lax.map(sketch_one, (dipole_all, blocks)).reshape(NDEV * RANK, MEMB)

    def target_step(total, items):
        near, reading_b, coupling_i, ranks_i, block, seen, count = items
        weights = coupling_i * rank_mask(ranks_i)
        combined = jnp.dot(weights, sketches, precision=highest, preferred_element_type=jnp.float32)
        near_pred = jnp.dot(block, near, preferred_element_type=jnp.float32)
        far_pred = lax.dot_general(combined.astype(jnp.bfloat16), reading_b, (((0,), (1,)), ((), ())), preferred_element_type=jnp.float32)
        valid = (jnp.arange(RDEV, dtype=jnp.int32) < count).astype(jnp.float32)
        residual = valid * (near_pred + far_pred - seen)
        rbits = residual.astype(jnp.bfloat16)
        near_grad = lax.dot_general(rbits, near, (((1,), (1,)), ((), ())), preferred_element_type=jnp.float32)
        transfer = lax.dot_general(reading_b, rbits, (((0,), (1,)), ((), ())), preferred_element_type=jnp.float32)
        parts = lax.dot_general(weights, transfer, (((0,), (0,)), ((), ())), precision=highest, preferred_element_type=jnp.float32)
        return total + parts, (residual, near_grad)

    start_total = jnp.zeros((NDEV * RANK, MEMB), jnp.float32)
    total, outputs = lax.scan(target_step, start_total, (near_all, reading_all, coupling_all, ranks_all, blocks, observed_all, counts_all))
    residuals, near_grads = outputs
    owners = total.reshape(NDEV, RANK, MEMB).astype(jnp.bfloat16)
    far_grads = lax.map(far_one, (owners, dipole_all))
    gradient = (near_grads + far_grads).reshape(N_LON, N_LAT, MEMB, 3, CLAT, CLON).transpose(2, 3, 1, 4, 0, 5).reshape(MEMB, 3, NLAT, NLON)
    new_moments = moments - step_size * smooth_field(gradient)
    misfit = residuals.reshape(N_LON, N_LAT, MEMB, RDEV).transpose(1, 0, 2, 3)
    return new_moments, misfit
```

```python
import functools

import jax
import jax.numpy as jnp
from jax import lax
from jax.experimental import pallas as pl
from jax.experimental.pallas import tpu as pltpu
from jax.sharding import PartitionSpec as P

step_size = 0.5
lat_limit = 1.25
MESH = pl.DeviceIdType.MESH
F32 = jnp.float32
BF16 = jnp.bfloat16

MEMB = 128
HALF = 64
ROWS = 48
ND = 6144
RDEV = 1024
RANK = 64
WIDE = 8192
PART_ROWS = (24, 24, 16)
PART_START = (0, 24, 48)
PART_AXES = ((0, 1, 2), (1, 2, 0), (2, 0, 1))
MCHUNK = 8
NCHUNK = 12
NROWS = ND // NCHUNK


def nt(a, b):
    return lax.dot_general(a, b, (((1,), (1,)), ((), ())), preferred_element_type=F32)


def nn(a, b):
    return jnp.dot(a, b, preferred_element_type=F32)


def exchange_kernel(
    mom, obs, counts, near, dip_t, read_t, coup, ranks,
    grad_out, mis_out, hn_out, hs_out, he_out, hw_out,
    mv, mbits, nearv, dpad, rpad, obsv, w_own, w_sib, wb, np_acc, rb, grad, sk, sk_in, comb, comb_in,
    tr, tr_in, own, own_in, edge_w, edge_e, hn, hs, he, hw,
    ag0, ag1, ag2, rs0, rs1, rs2, in0, in1, in2, two0, two1, two2, one0, one1, one2,
    ssem, rsem, lsem,
):
    ag, rs, rin = (ag0, ag1, ag2), (rs0, rs1, rs2), (in0, in1, in2)
    two, one = (two0, two1, two2), (one0, one1, one2)
    lon = lax.axis_index("lon")
    lat = lax.axis_index("lat")
    pos = (lon // 4, lon % 4, lat // 2)
    core = lat % 2
    mine = pl.multiple_of(core * HALF, HALF)
    other = pl.multiple_of((1 - core) * HALF, HALF)

    def along(axis, step):
        p = list(pos)
        p[axis] = (p[axis] + step) % 4
        return (p[0] * 4 + p[1], p[2] * 2 + core)

    sibling = (lon, pos[2] * 2 + 1 - core)
    north, south = (lon, (lat + 1) % 8), (lon, (lat + 7) % 8)
    east, west = ((lon + 1) % 16, lat), ((lon + 15) % 16, lat)

    peers = [sibling, north, south, east, west]
    peers += [along(axis, step) for axis in range(3) for step in (1, 2, 3)]
    barrier = pltpu.get_barrier_semaphore()
    for peer in peers:
        pl.semaphore_signal(barrier, inc=1, device_id=peer, device_id_type=MESH)

    used = [0, 0]
    sent = []

    def local(src, dst):
        copy = pltpu.make_async_copy(src, dst, lsem.at[used[0]])
        used[0] += 1
        copy.start()
        return copy

    def remote(src, dst, peer):
        copy = pltpu.make_async_remote_copy(
            src_ref=src, dst_ref=dst, send_sem=ssem.at[used[1]], recv_sem=rsem.at[used[1]],
            device_id=peer, device_id_type=MESH,
        )
        used[1] += 1
        copy.start()
        sent.append(copy)
        return copy

    msize = ND // MCHUNK
    mom_in = [local(mom.at[pl.ds(i * msize, msize)], mv.at[pl.ds(i * msize, msize)]) for i in range(MCHUNK)]
    dip_in = local(dip_t, dpad.at[pl.ds(mine, RANK)])
    coup_in = local(coup, w_own)
    read_in = local(read_t, rpad.at[pl.ds(mine, RANK)])
    obs_in = local(obs, obsv)
    dpad[pl.ds(other, RANK), :] = jnp.zeros((RANK, ND), BF16)
    rpad[pl.ds(other, RANK), :] = jnp.zeros((RANK, RDEV), BF16)
    members = MEMB // MCHUNK
    for i in range(MCHUNK):
        mom_in[i].wait()
        for r in range(ROWS):
            mbits[i * members:(i + 1) * members, r * 128:(r + 1) * 128] = mv[
                pl.ds(i * msize + r, members, stride=ROWS), :
            ].astype(BF16)
    near_in = [
        local(near.at[pl.ds(i * NROWS, NROWS)], nearv.at[pl.ds(i * NROWS, NROWS)]) for i in range(NCHUNK)
    ]
    dip_in.wait()
    sk[...] = nt(mbits[...], dpad[...])
    pl.semaphore_wait(barrier, len(peers))

    sk_copy = remote(sk.at[pl.ds(other, HALF)], sk_in, sibling)
    coup_in.wait()
    sk_copy.wait_recv()
    block = sk[pl.ds(mine, HALF), :] + sk_in[...]
    order = [[pos[a] for a in axes] for axes in PART_AXES]
    for p in range(3):
        k1, k2, k3 = order[p]
        ag[p][k3, k2, k1] = block[PART_START[p]:PART_START[p] + PART_ROWS[p]]

    first = []
    for p in range(3):
        k1, k2, k3 = order[p]
        for step in (1, 3, 2):
            first.append(remote(ag[p].at[k3, k2, k1], ag[p].at[k3, k2, k1], along(PART_AXES[p][0], step)))

    lane = lax.broadcasted_iota(jnp.int32, (RANK, 128), 1)
    row = lax.broadcasted_iota(jnp.int32, (RANK, 128), 0)
    inner = jnp.maximum(row, lane % RANK)

    def mask_step(q, _):
        cols = pl.ds(pl.multiple_of(q * 128, 128), 128)
        limit = jnp.where(lane < RANK, ranks[0, 2 * q], ranks[0, 2 * q + 1])
        value = jnp.where(inner < limit, w_own[:, cols], 0.0)
        w_own[:, cols] = value
        wb[pl.ds(mine, RANK), cols] = value.astype(BF16)
        return 0

    lax.fori_loop(0, 64, mask_step, 0)
    w_copy = remote(w_own, w_sib, sibling)

    def near_step(i):
        near_in[i].wait()
        part = nn(mbits[:, i * NROWS:(i + 1) * NROWS], nearv[i * NROWS:(i + 1) * NROWS, :])
        if i == 0:
            np_acc[...] = part
        else:
            np_acc[...] += part

    for i in range(3):
        near_step(i)
    for copy in first:
        copy.wait_recv()
    second = []
    for p in range(3):
        k1, k2, k3 = order[p]
        for step in (1, 3, 2):
            second.append(remote(ag[p].at[k3, k2], ag[p].at[k3, k2], along(PART_AXES[p][1], step)))
    for i in range(3, 7):
        near_step(i)
    for copy in second:
        copy.wait_recv()
    third_a, third_b, third_c = [], [], []
    lower, upper = pl.ds(0, 2), pl.ds(2, 2)
    for p in range(3):
        k3, axis = order[p][2], PART_AXES[p][2]
        third_a.append(remote(ag[p].at[k3, lower], ag[p].at[k3, lower], along(axis, 1)))
        third_a.append(remote(ag[p].at[k3, upper], ag[p].at[k3, upper], along(axis, 3)))
    for p in range(3):
        k3, axis = order[p][2], PART_AXES[p][2]
        third_b.append(remote(ag[p].at[k3, upper], ag[p].at[k3, upper], along(axis, 1)))
        third_b.append(remote(ag[p].at[k3, lower], ag[p].at[k3, lower], along(axis, 3)))
    for i in range(7, 9):
        near_step(i)
    for p in range(3):
        k3, axis = order[p][2], PART_AXES[p][2]
        before, after = (k3 + 3) % 4, (k3 + 1) % 4
        third_a[2 * p].wait_recv()
        third_c.append(remote(ag[p].at[before, lower], ag[p].at[before, lower], along(axis, 1)))
        third_a[2 * p + 1].wait_recv()
        third_c.append(remote(ag[p].at[after, upper], ag[p].at[after, upper], along(axis, 3)))
    w_copy.wait_recv()

    def sibling_step(q, _):
        cols = pl.ds(pl.multiple_of(q * 512, 512), 512)
        wb[pl.ds(other, RANK), cols] = w_sib[:, cols].astype(BF16)
        return 0

    lax.fori_loop(0, 16, sibling_step, 0)
    for i in range(9, NCHUNK):
        near_step(i)
    for copy in third_b + third_c:
        copy.wait_recv()

    def combine_step(q, total):
        qx, qy = q // 4, q % 4
        blocks = []
        for qz in range(4):
            blocks.append(jnp.concatenate([ag0[qz, qy, qx], ag1[qx, qz, qy], ag2[qy, qx, qz]], axis=0))
        value = jnp.concatenate(blocks, axis=1).astype(BF16)
        return total + nt(value, wb[:, pl.ds(pl.multiple_of(q * 512, 512), 512)])

    comb[...] = lax.fori_loop(0, 16, combine_step, jnp.zeros((HALF, 128), F32))
    comb_copy = remote(comb, comb_in, sibling)
    obs_in.wait()
    read_in.wait()
    comb_copy.wait_recv()
    valid = lax.broadcasted_iota(jnp.int32, (HALF, RDEV), 1) < counts[0, 0]
    for rows, source in ((mine, comb), (other, comb_in)):
        far = nn(source[...].astype(BF16), rpad[...])
        value = jnp.where(valid, np_acc[pl.ds(rows, HALF), :] + far - obsv[pl.ds(rows, HALF), :], 0.0)
        np_acc[pl.ds(rows, HALF), :] = value
        rb[pl.ds(rows, HALF), :] = value.astype(BF16)
    mis_copy = local(np_acc, mis_out)
    tr[...] = nt(rb[...], rpad[...])
    tr_copy = remote(tr.at[pl.ds(other, HALF)], tr_in, sibling)

    def grad_step(i):
        grad[:, i * NROWS:(i + 1) * NROWS] = nt(rb[...], nearv[i * NROWS:(i + 1) * NROWS, :])

    grad_step(0)
    tr_copy.wait_recv()
    pair = (tr[pl.ds(mine, HALF), :] + tr_in[...]).astype(BF16)

    def partial_step(q, _):
        qx, qy = q // 4, q % 4
        value = nn(pair, wb[:, pl.ds(pl.multiple_of(q * 512, 512), 512)])
        for qz in range(4):
            piece = value[:, qz * 128:(qz + 1) * 128]
            rs0[qz, qy, qx] = piece[0:24]
            rs1[qx, qz, qy] = piece[24:48]
            rs2[qy, qx, qz] = piece[48:64]
        return 0

    lax.fori_loop(0, 16, partial_step, 0)

    far_a, far_b, far_c = [], [], []
    for p in range(3):
        k3, axis = order[p][2], PART_AXES[p][2]
        opposite = (k3 + 2) % 4
        far_a.append(remote(rs[p].at[opposite, lower], rin[p].at[0], along(axis, 1)))
        far_a.append(remote(rs[p].at[opposite, upper], rin[p].at[1], along(axis, 3)))
    for p in range(3):
        k3, axis = order[p][2], PART_AXES[p][2]
        before, after = (k3 + 3) % 4, (k3 + 1) % 4
        far_b.append(remote(rs[p].at[after, upper], rin[p].at[2], along(axis, 1)))
        far_b.append(remote(rs[p].at[before, lower], rin[p].at[3], along(axis, 3)))
    for i in range(1, 4):
        grad_step(i)
    for p in range(3):
        k3, axis = order[p][2], PART_AXES[p][2]
        before, after = (k3 + 3) % 4, (k3 + 1) % 4
        far_a[2 * p].wait_recv()
        rs[p][after, lower] = rs[p][after, lower] + rin[p][0]
        far_c.append(remote(rs[p].at[after, lower], rin[p].at[4], along(axis, 1)))
        far_a[2 * p + 1].wait_recv()
        rs[p][before, upper] = rs[p][before, upper] + rin[p][1]
        far_c.append(remote(rs[p].at[before, upper], rin[p].at[5], along(axis, 3)))
    for i in range(4, 8):
        grad_step(i)
    for copy in far_b + far_c:
        copy.wait_recv()
    near_owner = []
    for p in range(3):
        k1, k2, k3 = order[p]
        rs[p][k3, lower] = rs[p][k3, lower] + rin[p][3] + rin[p][4]
        rs[p][k3, upper] = rs[p][k3, upper] + rin[p][2] + rin[p][5]
        for step in (1, 3, 2):
            near_owner.append(remote(rs[p].at[k3, (k2 + step) % 4], two[p].at[step - 1], along(PART_AXES[p][1], step)))
    for i in range(8, 10):
        grad_step(i)
    for copy in near_owner:
        copy.wait_recv()
    last = []
    for p in range(3):
        k1, k2, k3 = order[p]
        rs[p][k3, k2] = rs[p][k3, k2] + two[p][0] + two[p][1] + two[p][2]
        for step in (1, 3, 2):
            last.append(remote(rs[p].at[k3, k2, (k1 + step) % 4], one[p].at[step - 1], along(PART_AXES[p][0], step)))
    for i in range(10, NCHUNK):
        grad_step(i)
    for copy in last:
        copy.wait_recv()
    for p in range(3):
        k1, k2, k3 = order[p]
        own[PART_START[p]:PART_START[p] + PART_ROWS[p], :] = (
            rs[p][k3, k2, k1] + one[p][0] + one[p][1] + one[p][2]
        )
    own_copy = remote(own, own_in, sibling)
    own_copy.wait_recv()

    def far_grad(start, width):
        cols = pl.ds(start, width)
        for rows, source in ((mine, own), (other, own_in)):
            place = pl.ds(rows, HALF)
            grad[place, cols] = grad[place, cols] + nn(source[...].astype(BF16), dpad[:, cols])

    halo = []
    for layer in range(3):
        far_grad(layer * 2048, 128)
        far_grad(layer * 2048 + 15 * 128, 128)
        cols = pl.ds(layer * 128, 128)
        halo.append(remote(grad.at[:, pl.ds(layer * 2048, 128)], hn.at[:, cols], south))
        halo.append(remote(grad.at[:, pl.ds(layer * 2048 + 15 * 128, 128)], hs.at[:, cols], north))
    for layer in range(3):
        for start in (128, 1024):
            far_grad(layer * 2048 + start, 896)
    grad_copy = local(grad, grad_out)
    lanes = lax.broadcasted_iota(jnp.int32, (MEMB, 128), 1)
    first_col = jnp.zeros((MEMB, 128), F32)
    last_col = jnp.zeros((MEMB, 128), F32)
    for r in range(ROWS):
        value = grad[:, r * 128:(r + 1) * 128]
        turned = pltpu.roll(value, r, 1) if r else value
        first_col = jnp.where(lanes == r, turned, first_col)
        last_col = jnp.where(lanes == (r + 127) % 128, turned, last_col)
    edge_w[...] = first_col
    edge_e[...] = last_col
    halo.append(remote(edge_w, he, west))
    halo.append(remote(edge_e, hw, east))
    for copy in halo:
        copy.wait_recv()
    outs = [local(hn, hn_out), local(hs, hs_out), local(he, he_out), local(hw, hw_out)]
    for copy in sent:
        copy.wait_send()
    for copy in outs + [grad_copy, mis_copy]:
        copy.wait()


def smooth_kernel(mom, grad, hn, hs, he, hw, out, coef):
    members = grad.shape[0]

    @pl.when(pl.program_id(0) == 0)
    def _():
        lat = lax.axis_index("lat")
        row = lat * 16 + lax.broadcasted_iota(jnp.int32, (16, 128), 0)
        spacing = 2.0 * lat_limit / 128
        latitude = -lat_limit + (row.astype(F32) + 0.5) * spacing
        centre = jnp.cos(latitude)
        c_lon = 0.25 / (centre * centre)
        c_north = 0.25 * jnp.cos(latitude + 0.5 * spacing) / centre
        c_south = 0.25 * jnp.cos(latitude - 0.5 * spacing) / centre
        scale = step_size / (1.0 + c_north + c_south + 2.0 * c_lon)
        coef[0] = scale
        coef[1] = jnp.where(row < 127, scale * c_north, 0.0)
        coef[2] = jnp.where(row > 0, scale * c_south, 0.0)
        coef[3] = scale * c_lon

    lanes = lax.broadcasted_iota(jnp.int32, (members, 128), 1)
    for r in range(ROWS):
        layer, row = r // 16, r % 16
        here = grad[:, r * 128:(r + 1) * 128]
        cols = slice(layer * 128, (layer + 1) * 128)
        above = hn[:, cols] if row == 15 else grad[:, (r + 1) * 128:(r + 2) * 128]
        below = hs[:, cols] if row == 0 else grad[:, (r - 1) * 128:r * 128]
        right = jnp.where(lanes == 0, jnp.broadcast_to(he[:, r:r + 1], here.shape), here)
        col = (r + 127) % 128
        left = jnp.where(lanes == 127, jnp.broadcast_to(hw[:, col:col + 1], here.shape), here)
        sides = pltpu.roll(right, 127, 1) + pltpu.roll(left, 1, 1)
        change = (
            coef[0, row:row + 1, :] * here
            + coef[1, row:row + 1, :] * above
            + coef[2, row:row + 1, :] * below
            + coef[3, row:row + 1, :] * sides
        )
        place = pl.ds(r, members, stride=ROWS)
        out[place, :] = mom[place, :] - change


def shards(moments, observed, counts, near_kernel, dipole_basis, reading_basis, coupling, ranks):
    mom = moments.reshape(MEMB * ROWS, 128)
    hbm = pl.BlockSpec(memory_space=pl.ANY)
    smem = pl.BlockSpec(memory_space=pltpu.SMEM)
    vmem = pltpu.VMEM
    parts = PART_ROWS
    grad, misfit, hn, hs, he, hw = pl.pallas_call(
        exchange_kernel,
        out_shape=[
            jax.ShapeDtypeStruct((MEMB, ND), F32),
            jax.ShapeDtypeStruct((MEMB, RDEV), F32),
            jax.ShapeDtypeStruct((MEMB, 384), F32),
            jax.ShapeDtypeStruct((MEMB, 384), F32),
            jax.ShapeDtypeStruct((MEMB, 128), F32),
            jax.ShapeDtypeStruct((MEMB, 128), F32),
        ],
        in_specs=[hbm, hbm, smem, hbm, hbm, hbm, hbm, smem],
        out_specs=[hbm] * 6,
        scratch_shapes=[
            vmem((MEMB * ROWS, 128), F32),
            vmem((MEMB, ND), BF16),
            vmem((ND, RDEV), BF16),
            vmem((128, ND), BF16),
            vmem((128, RDEV), BF16),
            vmem((MEMB, RDEV), F32),
            vmem((RANK, WIDE), F32),
            vmem((RANK, WIDE), F32),
            vmem((128, WIDE), BF16),
            vmem((MEMB, RDEV), F32),
            vmem((MEMB, RDEV), BF16),
            vmem((MEMB, ND), F32),
            vmem((MEMB, 128), F32),
            vmem((HALF, 128), F32),
            vmem((HALF, 128), F32),
            vmem((HALF, 128), F32),
            vmem((MEMB, 128), F32),
            vmem((HALF, 128), F32),
            vmem((HALF, 128), F32),
            vmem((HALF, 128), F32),
            vmem((MEMB, 128), F32),
            vmem((MEMB, 128), F32),
            vmem((MEMB, 384), F32),
            vmem((MEMB, 384), F32),
            vmem((MEMB, 128), F32),
            vmem((MEMB, 128), F32),
        ]
        + [vmem((4, 4, 4, n, 128), F32) for n in parts]
        + [vmem((4, 4, 4, n, 128), F32) for n in parts]
        + [vmem((6, 2, 4, n, 128), F32) for n in parts]
        + [vmem((3, 4, n, 128), F32) for n in parts]
        + [vmem((3, n, 128), F32) for n in parts]
        + [pltpu.SemaphoreType.DMA((96,)), pltpu.SemaphoreType.DMA((96,)), pltpu.SemaphoreType.DMA((40,))],
        compiler_params=pltpu.CompilerParams(
            collective_id=0, has_side_effects=True, vmem_limit_bytes=60 * 1024 * 1024
        ),
        cost_estimate=pl.CostEstimate(flops=3_700_000_000, bytes_accessed=24_000_000, transcendentals=0),
        name="exchange",
    )(
        mom, observed[0, 0], counts, near_kernel[0, 0], dipole_basis[0, 0].T, reading_basis[0, 0].T,
        coupling[0, 0], ranks[0],
    )
    members = 16
    new = pl.pallas_call(
        smooth_kernel,
        grid=(MEMB // members,),
        out_shape=jax.ShapeDtypeStruct((MEMB * ROWS, 128), F32),
        in_specs=[
            pl.BlockSpec((members * ROWS, 128), lambda i: (i, 0)),
            pl.BlockSpec((members, ND), lambda i: (i, 0)),
            pl.BlockSpec((members, 384), lambda i: (i, 0)),
            pl.BlockSpec((members, 384), lambda i: (i, 0)),
            pl.BlockSpec((members, 128), lambda i: (i, 0)),
            pl.BlockSpec((members, 128), lambda i: (i, 0)),
        ],
        out_specs=pl.BlockSpec((members * ROWS, 128), lambda i: (i, 0)),
        scratch_shapes=[vmem((4, 16, 128), F32)],
        compiler_params=pltpu.CompilerParams(vmem_limit_bytes=32 * 1024 * 1024),
        cost_estimate=pl.CostEstimate(flops=10_000_000, bytes_accessed=9_500_000, transcendentals=0),
        name="smooth",
    )(mom, grad, hn, hs, he, hw)
    return new.reshape(moments.shape), misfit[None, None]


def solution(mesh):
    return jax.shard_map(
        shards,
        mesh=mesh,
        in_specs=(
            P(None, None, "lat", "lon"),
            P("lat", "lon", None, None),
            P("lat", "lon"),
            P("lat", "lon", None, None),
            P("lat", "lon", None, None),
            P("lat", "lon", None, None),
            P("lat", "lon", None, None),
            P("lat", "lon", None),
        ),
        out_specs=(P(None, None, "lat", "lon"), P("lat", "lon", None, None)),
        check_vma=False,
    )
```

```python
import functools

import jax
import jax.numpy as jnp
from jax import lax
from jax.experimental import pallas as pl
from jax.experimental.pallas import tpu as pltpu
from jax.sharding import PartitionSpec as P

step_size = 0.5
lat_limit = 1.25
MESH = pl.DeviceIdType.MESH
F32 = jnp.float32
BF16 = jnp.bfloat16

MEMB = 128
HALF = 64
ROWS = 48
ND = 6144
RDEV = 1024
RANK = 64
WIDE = 8192
PART_ROWS = (16, 24, 24)
PART_START = (0, 16, 40)
PART_AXES = ((0, 1, 2), (1, 2, 0), (2, 0, 1))
MCHUNK = 8
NCHUNK = 12
NROWS = ND // NCHUNK


def nt(a, b):
    return lax.dot_general(a, b, (((1,), (1,)), ((), ())), preferred_element_type=F32)


def nn(a, b):
    return jnp.dot(a, b, preferred_element_type=F32)


def exchange_kernel(
    mom, obs, counts, near, dip_t, read_t, coup, ranks,
    grad, mv, mis, halo_out,
    mbits, nearv, dpad, rpad, obsv, w_own, w_sib, wb, rb, sk, sk_in, comb, comb_in,
    tr, tr_in, own, own_in, edge_w, edge_e, base_w, base_e, hn, hs, he, hw,
    ag0, ag1, ag2, rs0, rs1, rs2, in0, in1, in2, two0, two1, two2, one0, one1, one2,
    ssem, rsem, lsem,
):
    ag, rs, rin = (ag0, ag1, ag2), (rs0, rs1, rs2), (in0, in1, in2)
    two, one = (two0, two1, two2), (one0, one1, one2)
    lon = lax.axis_index("lon")
    lat = lax.axis_index("lat")
    pos = (lon // 4, lon % 4, lat // 2)
    core = lat % 2
    mine = pl.multiple_of(core * HALF, HALF)
    other = pl.multiple_of((1 - core) * HALF, HALF)

    def along(axis, step):
        p = list(pos)
        p[axis] = (p[axis] + step) % 4
        return (p[0] * 4 + p[1], p[2] * 2 + core)

    sibling = (lon, pos[2] * 2 + 1 - core)
    north, south = (lon, (lat + 1) % 8), (lon, (lat + 7) % 8)
    east, west = ((lon + 1) % 16, lat), ((lon + 15) % 16, lat)

    peers = [sibling, north, south, east, west]
    peers += [along(axis, step) for axis in range(3) for step in (1, 2, 3)]
    barrier = pltpu.get_barrier_semaphore()
    for peer in peers:
        pl.semaphore_signal(barrier, inc=1, device_id=peer, device_id_type=MESH)

    used = [0, 0]
    sent = []

    def local(src, dst):
        copy = pltpu.make_async_copy(src, dst, lsem.at[used[0]])
        used[0] += 1
        copy.start()
        return copy

    def remote(src, dst, peer):
        copy = pltpu.make_async_remote_copy(
            src_ref=src, dst_ref=dst, send_sem=ssem.at[used[1]], recv_sem=rsem.at[used[1]],
            device_id=peer, device_id_type=MESH,
        )
        used[1] += 1
        copy.start()
        sent.append(copy)
        return copy

    msize = ND // MCHUNK
    for i in range(MCHUNK):
        local(mom.at[pl.ds(i * msize, msize)], mv.at[pl.ds(i * msize, msize)])
    dip_in = local(dip_t, dpad.at[pl.ds(mine, RANK)])
    coup_in = local(coup, w_own)
    read_in = local(read_t, rpad.at[pl.ds(mine, RANK)])
    obs_in = local(obs, obsv)
    dpad[pl.ds(other, RANK), :] = jnp.zeros((RANK, ND), BF16)
    rpad[pl.ds(other, RANK), :] = jnp.zeros((RANK, RDEV), BF16)
    members = MEMB // MCHUNK

    def cast_step(i, _):
        start = pl.multiple_of(i * msize, msize)
        pltpu.make_async_copy(mom.at[pl.ds(start, msize)], mv.at[pl.ds(start, msize)], lsem.at[i]).wait()
        for r in range(ROWS):
            mbits[pl.ds(pl.multiple_of(i * members, members), members), r * 128:(r + 1) * 128] = mv[
                pl.ds(start + r, members, stride=ROWS), :
            ].astype(BF16)
        return 0

    lax.fori_loop(0, MCHUNK, cast_step, 0)
    dip_in.wait()
    sk[...] = nt(mbits[...], dpad[...])
    pl.semaphore_wait(barrier, len(peers))

    sk_copy = remote(sk.at[pl.ds(other, HALF)], sk_in, sibling)
    near_in = [
        local(near.at[pl.ds(i * NROWS, NROWS)], nearv.at[pl.ds(i * NROWS, NROWS)]) for i in range(NCHUNK)
    ]
    sk_copy.wait_recv()
    block = sk[pl.ds(mine, HALF), :] + sk_in[...]
    for p in range(3):
        ag[p][0, 0, 0] = block[PART_START[p]:PART_START[p] + PART_ROWS[p]]

    first = []
    for step in (2, 1, 3):
        for p in range(3):
            first.append(remote(ag[p].at[0, 0, 0], ag[p].at[0, 0, 4 - step], along(PART_AXES[p][0], step)))

    coup_in.wait()
    lane = lax.broadcasted_iota(jnp.int32, (RANK, 128), 1)
    row = lax.broadcasted_iota(jnp.int32, (RANK, 128), 0)
    inner = jnp.maximum(row, lane % RANK)

    def split(value):
        upper = value.astype(BF16)
        return upper, (value - upper.astype(F32)).astype(BF16)

    def mask_step(q, _):
        cols = pl.ds(pl.multiple_of(q * 128, 128), 128)
        limit = jnp.where(lane < RANK, ranks[0, 2 * q], ranks[0, 2 * q + 1])
        value = jnp.where(inner < limit, w_own[:, cols], 0.0)
        w_own[:, cols] = value
        upper, rest = split(value)
        wb[pl.ds(mine, RANK), cols] = upper
        wb[pl.ds(128 + mine, RANK), cols] = rest
        return 0

    lax.fori_loop(0, 64, mask_step, 0)
    w_copy = remote(w_own, w_sib, sibling)

    def near_step(i):
        near_in[i].wait()
        part = nn(mbits[:, i * NROWS:(i + 1) * NROWS], nearv[i * NROWS:(i + 1) * NROWS, :])
        if i == 0:
            mis[...] = part
        else:
            mis[...] += part

    near_step(0)
    for copy in first:
        copy.wait_recv()
    second = []
    for step in (2, 1, 3):
        for p in range(3):
            second.append(remote(ag[p].at[0, 0], ag[p].at[0, 4 - step], along(PART_AXES[p][1], step)))
    early = []
    for p in range(3):
        axis = PART_AXES[p][2]
        early.append(remote(ag[p].at[0, 0], ag[p].at[3, 0], along(axis, 1)))
        early.append(remote(ag[p].at[0, 0], ag[p].at[1, 0], along(axis, 3)))
    for i in range(1, 3):
        near_step(i)
    for copy in second:
        copy.wait_recv()
    third, relay, rest = [], [], []
    for p in range(3):
        axis = PART_AXES[p][2]
        third.append(remote(ag[p].at[0, 1], ag[p].at[3, 1], along(axis, 1)))
        third.append(remote(ag[p].at[0, 2], ag[p].at[1, 2], along(axis, 3)))
        third.append(remote(ag[p].at[0, 3], ag[p].at[1, 3], along(axis, 3)))
    for p in range(3):
        early[2 * p].wait_recv()
        relay.append(remote(ag[p].at[3, 0], ag[p].at[2, 0], along(PART_AXES[p][2], 1)))
    for p in range(3):
        axis = PART_AXES[p][2]
        rest.append(remote(ag[p].at[0, pl.ds(2, 2)], ag[p].at[3, pl.ds(2, 2)], along(axis, 1)))
        rest.append(remote(ag[p].at[0, 1], ag[p].at[1, 1], along(axis, 3)))
    for i in range(3, 6):
        near_step(i)
    for p in range(3):
        axis = PART_AXES[p][2]
        third[3 * p].wait_recv()
        relay.append(remote(ag[p].at[3, 1], ag[p].at[2, 1], along(axis, 1)))
        third[3 * p + 1].wait_recv()
        relay.append(remote(ag[p].at[1, 2], ag[p].at[2, 2], along(axis, 3)))
    for p in range(3):
        third[3 * p + 2].wait_recv()
        relay.append(remote(ag[p].at[1, 3], ag[p].at[2, 3], along(PART_AXES[p][2], 3)))
    w_copy.wait_recv()

    def sibling_step(q, _):
        cols = pl.ds(pl.multiple_of(q * 512, 512), 512)
        upper, rest = split(w_sib[:, cols])
        wb[pl.ds(other, RANK), cols] = upper
        wb[pl.ds(128 + other, RANK), cols] = rest
        return 0

    lax.fori_loop(0, 16, sibling_step, 0)
    for i in range(6, NCHUNK):
        near_step(i)
    for p in range(3):
        early[2 * p + 1].wait_recv()
    for copy in rest + relay:
        copy.wait_recv()

    def columns(ax, ay):
        q = (pos[0] + ax) % 4 * 16 + (pos[1] + ay) % 4 * 4
        return pl.ds(pl.multiple_of(q * 128, 512), 512)

    total = None
    for ax in range(4):
        for ay in range(4):
            blocks = []
            for qz in range(4):
                az = (qz + 4 - pos[2]) % 4
                blocks.append(jnp.concatenate([ag0[az, ay, ax], ag1[ax, az, ay], ag2[ay, ax, az]], axis=0))
            upper, rest = split(jnp.concatenate(blocks, axis=1))
            part = nt(jnp.concatenate([upper, rest], axis=0), wb[:, columns(ax, ay)])
            total = part if total is None else total + part
    comb[...] = total[:HALF, :128] + (total[:HALF, 128:] + total[HALF:, :128])
    comb_copy = remote(comb, comb_in, sibling)
    obs_in.wait()
    read_in.wait()
    comb_copy.wait_recv()
    valid = lax.broadcasted_iota(jnp.int32, (HALF, RDEV), 1) < counts[0, 0]
    for rows, source in ((mine, comb), (other, comb_in)):
        far = nn(source[...].astype(BF16), rpad[...])
        value = jnp.where(valid, mis[pl.ds(rows, HALF), :] + far - obsv[pl.ds(rows, HALF), :], 0.0)
        mis[pl.ds(rows, HALF), :] = value
        rb[pl.ds(rows, HALF), :] = value.astype(BF16)
    tr[...] = nt(rb[...], rpad[...])
    tr_copy = remote(tr.at[pl.ds(other, HALF)], tr_in, sibling)

    lanes = lax.broadcasted_iota(jnp.int32, (MEMB, 128), 1)

    def edge_cols(array, start, stop, low, high):
        for r in range(start, stop):
            value = array[:, r * 128:(r + 1) * 128].astype(F32)
            turned = pltpu.roll(value, r, 1) if r else value
            low = jnp.where(lanes == r, turned, low)
            high = jnp.where(lanes == (r + 127) % 128, turned, high)
        return low, high

    blank = jnp.zeros((MEMB, 128), F32)

    def grad_step(i):
        grad[:, i * NROWS:(i + 1) * NROWS] = nt(rb[...], nearv[i * NROWS:(i + 1) * NROWS, :])

    low, high = edge_cols(dpad, 0, ROWS, blank, blank)
    base_w[...] = low.astype(BF16)
    base_e[...] = high.astype(BF16)
    tr_copy.wait_recv()
    upper, rest = split(tr[pl.ds(mine, HALF), :] + tr_in[...])
    pair = jnp.concatenate(
        [jnp.concatenate([upper, upper], axis=1), jnp.concatenate([rest, jnp.zeros_like(rest)], axis=1)], axis=0
    )

    def partial_step(ax, ay):
        value = nn(pair, wb[:, columns(ax, ay)])
        value = value[:HALF] + value[HALF:]
        for qz in range(4):
            az = (qz + 4 - pos[2]) % 4
            piece = value[:, qz * 128:(qz + 1) * 128]
            rs0[az, ay, ax] = piece[PART_START[0]:PART_START[1]]
            rs1[ax, az, ay] = piece[PART_START[1]:PART_START[2]]
            rs2[ay, ax, az] = piece[PART_START[2]:]

    opp = {}

    def send_opposite(p):
        axis = PART_AXES[p][2]
        opp[p, 1] = remote(rs[p].at[2, 1], rin[p].at[0], along(axis, 1))
        opp[p, 2] = remote(rs[p].at[2, 2], rin[p].at[1], along(axis, 3))
        opp[p, 3] = remote(rs[p].at[2, 3], rin[p].at[2], along(axis, 3))

    for ay in range(4):
        partial_step(2, ay)
    send_opposite(1)
    for ax in (0, 1, 3):
        partial_step(ax, 2)
    send_opposite(2)
    for ax in (0, 1, 3):
        for ay in (0, 1, 3):
            partial_step(ax, ay)
    send_opposite(0)
    direct = []
    for p in (1, 2, 0):
        axis = PART_AXES[p][2]
        direct.append(remote(rs[p].at[1, pl.ds(2, 2)], rin[p].at[pl.ds(4, 2)], along(axis, 1)))
        direct.append(remote(rs[p].at[3, 1], rin[p].at[3], along(axis, 3)))
        opp[p, 0] = remote(rs[p].at[2, 0], rin[p].at[6], along(axis, 1))
    for i in range(0, 3):
        grad_step(i)
    dep, late = [], []
    for p in (1, 2, 0):
        axis = PART_AXES[p][2]
        opp[p, 1].wait_recv()
        rs[p][1, 1] = rs[p][1, 1] + rin[p][0]
        dep.append(remote(rs[p].at[1, 1], rin[p].at[7], along(axis, 1)))
        opp[p, 2].wait_recv()
        rs[p][3, 2] = rs[p][3, 2] + rin[p][1]
        dep.append(remote(rs[p].at[3, 2], rin[p].at[8], along(axis, 3)))
    for p in (1, 2, 0):
        opp[p, 3].wait_recv()
        rs[p][3, 3] = rs[p][3, 3] + rin[p][2]
        dep.append(remote(rs[p].at[3, 3], rin[p].at[9], along(PART_AXES[p][2], 3)))
    for p in (1, 2, 0):
        axis = PART_AXES[p][2]
        late.append(remote(rs[p].at[3, 0], rin[p].at[10], along(axis, 3)))
        opp[p, 0].wait_recv()
        rs[p][1, 0] = rs[p][1, 0] + rin[p][6]
        late.append(remote(rs[p].at[1, 0], rin[p].at[11], along(axis, 1)))
    for i in range(3, 10):
        grad_step(i)
    for copy in direct + dep:
        copy.wait_recv()
    near_owner = []
    for p in range(3):
        rs[p][0, 2] = rs[p][0, 2] + rin[p][4] + rin[p][8]
        near_owner.append(remote(rs[p].at[0, 2], two[p].at[1], along(PART_AXES[p][1], 2)))
    for p in range(3):
        rs[p][0, 1] = rs[p][0, 1] + rin[p][3] + rin[p][7]
        near_owner.append(remote(rs[p].at[0, 1], two[p].at[0], along(PART_AXES[p][1], 1)))
        rs[p][0, 3] = rs[p][0, 3] + rin[p][5] + rin[p][9]
        near_owner.append(remote(rs[p].at[0, 3], two[p].at[2], along(PART_AXES[p][1], 3)))
    for i in range(10, NCHUNK):
        grad_step(i)
    for copy in late:
        copy.wait_recv()
    for p in range(3):
        rs[p][0, 0] = rs[p][0, 0] + rin[p][10] + rin[p][11]
    for copy in near_owner:
        copy.wait_recv()
    last = []
    for p in range(3):
        rs[p][0, 0] = rs[p][0, 0] + two[p][0] + two[p][1] + two[p][2]
    for step in (2, 1, 3):
        for p in range(3):
            last.append(remote(rs[p].at[0, 0, step], one[p].at[step - 1], along(PART_AXES[p][0], step)))
    low, high = edge_cols(grad, 0, ROWS, blank, blank)
    edge_w[...] = low
    edge_e[...] = high
    for copy in last:
        copy.wait_recv()
    for p in range(3):
        own[PART_START[p]:PART_START[p] + PART_ROWS[p], :] = (
            rs[p][0, 0, 0] + one[p][0] + one[p][1] + one[p][2]
        )
    own_copy = remote(own, own_in, sibling)
    own_copy.wait_recv()

    def far(where, base):
        for rows, source in ((mine, own), (other, own_in)):
            place = pl.ds(rows, HALF)
            where[place, :] = where[place, :] + nn(source[...].astype(BF16), base)

    def far_grad(start, width):
        far(grad.at[:, pl.ds(start, width)], dpad[:, pl.ds(start, width)])

    far(edge_w, base_w[...])
    far(edge_e, base_e[...])
    halo = [remote(edge_w, he, west), remote(edge_e, hw, east)]
    for layer in range(3):
        cols = pl.ds(layer * 128, 128)
        start = layer * 2048
        far_grad(start, 128)
        halo.append(remote(grad.at[:, pl.ds(start, 128)], hn.at[:, cols], south))
        far_grad(start + 15 * 128, 128)
        halo.append(remote(grad.at[:, pl.ds(start + 15 * 128, 128)], hs.at[:, cols], north))
    for layer in range(3):
        for start in (128, 1024):
            far_grad(layer * 2048 + start, 896)
    for copy in halo:
        copy.wait_recv()
    halo_out[:, 0:384] = hn[...]
    halo_out[:, 384:768] = hs[...]
    halo_out[:, 768:896] = he[...]
    halo_out[:, 896:1024] = hw[...]
    for copy in sent:
        copy.wait_send()


def smooth_kernel(mom, grad, mis, halo, out, mis_out, coef):
    members = mis_out.shape[0]
    step = pl.program_id(0)

    @pl.when(step == 0)
    def _():
        lat = lax.axis_index("lat")
        row = lat * 16 + lax.broadcasted_iota(jnp.int32, (16, 128), 0)
        spacing = 2.0 * lat_limit / 128
        latitude = -lat_limit + (row.astype(F32) + 0.5) * spacing
        centre = jnp.cos(latitude)
        c_lon = 0.25 / (centre * centre)
        c_north = 0.25 * jnp.cos(latitude + 0.5 * spacing) / centre
        c_south = 0.25 * jnp.cos(latitude - 0.5 * spacing) / centre
        scale = step_size / (1.0 + c_north + c_south + 2.0 * c_lon)
        coef[0] = scale
        coef[1] = jnp.where(row < 127, scale * c_north, 0.0)
        coef[2] = jnp.where(row > 0, scale * c_south, 0.0)
        coef[3] = scale * c_lon

    mine = pl.ds(pl.multiple_of(step * members, members), members)
    mis_out[...] = mis[mine, :]
    lanes = lax.broadcasted_iota(jnp.int32, (members, 128), 1)
    from_east = halo[mine, 768:896]
    from_west = halo[mine, 896:1024]
    for r in range(ROWS):
        layer, row = r // 16, r % 16
        here = grad[mine, r * 128:(r + 1) * 128]
        above = (
            halo[mine, layer * 128:(layer + 1) * 128] if row == 15 else grad[mine, (r + 1) * 128:(r + 2) * 128]
        )
        below = (
            halo[mine, 384 + layer * 128:384 + (layer + 1) * 128] if row == 0 else grad[mine, (r - 1) * 128:r * 128]
        )
        right = jnp.where(lanes == 127, pltpu.roll(from_east, 127 - r, 1), pltpu.roll(here, 127, 1))
        left = jnp.where(lanes == 0, pltpu.roll(from_west, (129 - r) % 128, 1), pltpu.roll(here, 1, 1))
        change = (
            coef[0, row:row + 1, :] * here
            + coef[1, row:row + 1, :] * above
            + coef[2, row:row + 1, :] * below
            + coef[3, row:row + 1, :] * (right + left)
        )
        out[pl.ds(r, members, stride=ROWS), :] = mom[pl.ds(step * (members * ROWS) + r, members, stride=ROWS), :] - change


def shards(moments, observed, counts, near_kernel, dipole_basis, reading_basis, coupling, ranks):
    mom = moments.reshape(MEMB * ROWS, 128)
    hbm = pl.BlockSpec(memory_space=pl.ANY)
    smem = pl.BlockSpec(memory_space=pltpu.SMEM)
    whole = pl.BlockSpec(memory_space=pltpu.VMEM)
    vmem = pltpu.VMEM
    parts = PART_ROWS
    grad, loaded, misfit, halo = pl.pallas_call(
        exchange_kernel,
        out_shape=[
            vmem((MEMB, ND), F32),
            vmem((MEMB * ROWS, 128), F32),
            vmem((MEMB, RDEV), F32),
            vmem((MEMB, 1024), F32),
        ],
        in_specs=[hbm, hbm, smem, hbm, hbm, hbm, hbm, smem],
        out_specs=[whole] * 4,
        scratch_shapes=[
            vmem((MEMB, ND), BF16),
            vmem((ND, RDEV), BF16),
            vmem((128, ND), BF16),
            vmem((128, RDEV), BF16),
            vmem((MEMB, RDEV), F32),
            vmem((RANK, WIDE), F32),
            vmem((RANK, WIDE), F32),
            vmem((256, WIDE), BF16),
            vmem((MEMB, RDEV), BF16),
            vmem((MEMB, 128), F32),
            vmem((HALF, 128), F32),
            vmem((HALF, 128), F32),
            vmem((HALF, 128), F32),
            vmem((MEMB, 128), F32),
            vmem((HALF, 128), F32),
            vmem((HALF, 128), F32),
            vmem((HALF, 128), F32),
            vmem((MEMB, 128), F32),
            vmem((MEMB, 128), F32),
            vmem((128, 128), BF16),
            vmem((128, 128), BF16),
            vmem((MEMB, 384), F32),
            vmem((MEMB, 384), F32),
            vmem((MEMB, 128), F32),
            vmem((MEMB, 128), F32),
        ]
        + [vmem((4, 4, 4, n, 128), F32) for n in parts]
        + [vmem((4, 4, 4, n, 128), F32) for n in parts]
        + [vmem((12, 4, n, 128), F32) for n in parts]
        + [vmem((3, 4, n, 128), F32) for n in parts]
        + [vmem((3, n, 128), F32) for n in parts]
        + [pltpu.SemaphoreType.DMA((128,)), pltpu.SemaphoreType.DMA((128,)), pltpu.SemaphoreType.DMA((40,))],
        compiler_params=pltpu.CompilerParams(
            collective_id=0, has_side_effects=True, vmem_limit_bytes=48 * 1024 * 1024
        ),
        cost_estimate=pl.CostEstimate(flops=3_700_000_000, bytes_accessed=24_000_000, transcendentals=0),
        name="exchange",
    )(
        mom, observed[0, 0], counts, near_kernel[0, 0], dipole_basis[0, 0].T, reading_basis[0, 0].T,
        coupling[0, 0], ranks[0],
    )
    members = 16
    new, misfit = pl.pallas_call(
        smooth_kernel,
        grid=(MEMB // members,),
        out_shape=[
            jax.ShapeDtypeStruct((MEMB * ROWS, 128), F32),
            jax.ShapeDtypeStruct((MEMB, RDEV), F32),
        ],
        in_specs=[whole] * 4,
        out_specs=[
            pl.BlockSpec((members * ROWS, 128), lambda i: (i, 0)),
            pl.BlockSpec((members, RDEV), lambda i: (i, 0)),
        ],
        scratch_shapes=[vmem((4, 16, 128), F32)],
        compiler_params=pltpu.CompilerParams(vmem_limit_bytes=32 * 1024 * 1024),
        cost_estimate=pl.CostEstimate(flops=10_000_000, bytes_accessed=4_000_000, transcendentals=0),
        name="smooth",
    )(loaded, grad, misfit, halo)
    return new.reshape(moments.shape), misfit[None, None]


def solution(mesh):
    return jax.shard_map(
        shards,
        mesh=mesh,
        in_specs=(
            P(None, None, "lat", "lon"),
            P("lat", "lon", None, None),
            P("lat", "lon"),
            P("lat", "lon", None, None),
            P("lat", "lon", None, None),
            P("lat", "lon", None, None),
            P("lat", "lon", None, None),
            P("lat", "lon", None),
        ),
        out_specs=(P(None, None, "lat", "lon"), P("lat", "lon", None, None)),
        check_vma=False,
    )
```

```python
import functools

import jax
import jax.numpy as jnp
from jax import lax
from jax.experimental import pallas as pl
from jax.experimental.pallas import tpu as pltpu
from jax.sharding import PartitionSpec as P

step_size = 0.5
lat_limit = 1.25
MESH = pl.DeviceIdType.MESH
F32 = jnp.float32
BF16 = jnp.bfloat16

MEMB = 128
HALF = 64
ROWS = 48
ND = 6144
RDEV = 1024
RANK = 64
WIDE = 8192
PART_ROWS = (16, 24, 24)
PART_START = (0, 16, 40)
PART_AXES = ((0, 1, 2), (1, 2, 0), (2, 0, 1))
MCHUNK = 8
SENDS = 32
RECVS = 73
NCHUNK = 12
NROWS = ND // NCHUNK


def nt(a, b):
    return lax.dot_general(a, b, (((1,), (1,)), ((), ())), preferred_element_type=F32)


def nn(a, b):
    return jnp.dot(a, b, preferred_element_type=F32)


def exchange_kernel(
    mom, obs, counts, near, dip_t, read_t, coup, ranks,
    grad_out, mom_out, mis_out, halo_out, coef_out,
    grad, mv, mis, halo, coef, wt,
    mbits, nearv, dpad, rpad, obsv, w_own, w_sib, wb, rb, sk, sk_in, comb, comb_in,
    tr, tr_in, own, edge_w, edge_e, base_w, base_e, hn, hs, he, hw,
    ag0, ag1, ag2, rs0, rs1, rs2, in0, in1, in2, two0, two1, two2, one0, one1, one2,
    far0, far1, far2, same0, same1, same2, cross0, cross1, cross2,
    ssem, rsem, lsem,
):
    ag, rs, rin = (ag0, ag1, ag2), (rs0, rs1, rs2), (in0, in1, in2)
    two, one, far_one = (two0, two1, two2), (one0, one1, one2), (far0, far1, far2)
    same, cross = (same0, same1, same2), (cross0, cross1, cross2)
    lon = lax.axis_index("lon")
    lat = lax.axis_index("lat")
    pos = (lon // 4, lon % 4, lat // 2)
    core = lat % 2
    mine = pl.multiple_of(core * HALF, HALF)
    other = pl.multiple_of((1 - core) * HALF, HALF)

    def along(axis, step, on=core):
        p = list(pos)
        p[axis] = (p[axis] + step) % 4
        return (p[0] * 4 + p[1], p[2] * 2 + on)

    sibling = (lon, pos[2] * 2 + 1 - core)
    north, south = (lon, (lat + 1) % 8), (lon, (lat + 7) % 8)
    east, west = ((lon + 1) % 16, lat), ((lon + 15) % 16, lat)

    peers = [sibling, north, south, east, west]
    peers += [along(axis, step, on) for axis in range(3) for step in (1, 2, 3) for on in (core, 1 - core)]
    barrier = pltpu.get_barrier_semaphore()
    for peer in peers:
        pl.semaphore_signal(barrier, inc=1, device_id=peer, device_id_type=MESH)

    used = [0, 0, 0]
    sent = []

    def local(src, dst):
        copy = pltpu.make_async_copy(src, dst, lsem.at[used[0]])
        used[0] += 1
        copy.start()
        return copy

    def remote(src, dst, peer):
        if len(sent) >= SENDS:
            sent[-SENDS].wait_send()
        copy = pltpu.make_async_remote_copy(
            src_ref=src, dst_ref=dst, send_sem=ssem.at[len(sent) % SENDS], recv_sem=rsem.at[used[1]],
            device_id=peer, device_id_type=MESH,
        )
        used[1] += 1
        used[2] = max(used[2], used[1])
        copy.start()
        sent.append(copy)
        return copy

    msize = ND // MCHUNK
    mom_in = [local(mom.at[pl.ds(i * msize, msize)], mv.at[pl.ds(i * msize, msize)]) for i in range(MCHUNK)]
    used[0] = 12
    dip_in = local(dip_t, dpad.at[pl.ds(mine, RANK)])
    coup_in = local(coup, w_own)
    read_in = local(read_t, rpad.at[pl.ds(mine, RANK)])
    obs_in = local(obs, obsv)
    dpad[pl.ds(other, RANK), :] = jnp.zeros((RANK, ND), BF16)
    rpad[pl.ds(other, RANK), :] = jnp.zeros((RANK, RDEV), BF16)
    members = MEMB // MCHUNK

    for i in range(MCHUNK):
        mom_in[i].wait()
        for r in range(ROWS):
            mbits[i * members:(i + 1) * members, r * 128:(r + 1) * 128] = mv[
                pl.ds(i * msize + r, members, stride=ROWS), :
            ].astype(BF16)
    dip_in.wait()
    sk[...] = nt(mbits[...], dpad[...])
    pl.semaphore_wait(barrier, len(peers))

    sk_copy = remote(sk.at[pl.ds(other, HALF)], sk_in, sibling)
    first = []
    for step in (2, 1, 3):
        for p in range(3):
            for on, rows, place in ((core, mine, same[p]), (1 - core, other, cross[p])):
                source = sk.at[pl.ds(pl.multiple_of(rows + PART_START[p], 8), PART_ROWS[p])]
                first.append(remote(source, place.at[step - 1], along(PART_AXES[p][0], step, on)))
    used[0] = 0
    near_in = [
        local(near.at[pl.ds(i * NROWS, NROWS)], nearv.at[pl.ds(i * NROWS, NROWS)]) for i in range(NCHUNK)
    ]

    coup_in.wait()
    lane = lax.broadcasted_iota(jnp.int32, (RANK, 128), 1)
    row = lax.broadcasted_iota(jnp.int32, (RANK, 128), 0)
    inner = jnp.maximum(row, lane % RANK)

    def split(value):
        upper = value.astype(BF16)
        return upper, (value - upper.astype(F32)).astype(BF16)

    def mask_step(q, _):
        cols = pl.ds(pl.multiple_of(q * 128, 128), 128)
        limit = jnp.where(lane < RANK, ranks[0, 2 * q], ranks[0, 2 * q + 1])
        value = jnp.where(inner < limit, w_own[:, cols], 0.0)
        w_own[:, cols] = value
        upper, rest = split(value)
        wb[pl.ds(mine, RANK), cols] = upper
        wb[pl.ds(128 + mine, RANK), cols] = rest
        return 0

    lax.fori_loop(0, 24, mask_step, 0)

    def near_step(i):
        near_in[i].wait()
        part = nn(mbits[:, i * NROWS:(i + 1) * NROWS], nearv[i * NROWS:(i + 1) * NROWS, :])
        if i == 0:
            mis[...] = part
        else:
            mis[...] += part

    sk_copy.wait_recv()
    block = sk[pl.ds(mine, HALF), :] + sk_in[...]
    for p in range(3):
        ag[p][0, 0, 0] = block[PART_START[p]:PART_START[p] + PART_ROWS[p]]
    for copy in first:
        copy.wait_recv()
    for p in range(3):
        for step in (1, 2, 3):
            ag[p][0, 0, 4 - step] = same[p][step - 1] + cross[p][step - 1]
    second = []
    for step in (2, 1, 3):
        for p in range(3):
            second.append(remote(ag[p].at[0, 0], ag[p].at[0, 4 - step], along(PART_AXES[p][1], step)))
    early = []
    for p in range(3):
        axis = PART_AXES[p][2]
        early.append(remote(ag[p].at[0, 0], ag[p].at[3, 0], along(axis, 1)))
        early.append(remote(ag[p].at[0, 0], ag[p].at[1, 0], along(axis, 3)))
    lax.fori_loop(24, 64, mask_step, 0)
    w_copy = remote(w_own, w_sib, sibling)
    for i in range(0, 2):
        near_step(i)
    for copy in second:
        copy.wait_recv()
    third, relay, rest = [], [], []
    for p in range(3):
        axis = PART_AXES[p][2]
        third.append(remote(ag[p].at[0, 1], ag[p].at[3, 1], along(axis, 1)))
        third.append(remote(ag[p].at[0, 2], ag[p].at[1, 2], along(axis, 3)))
        third.append(remote(ag[p].at[0, 3], ag[p].at[1, 3], along(axis, 3)))
    for p in range(3):
        early[2 * p].wait_recv()
        relay.append(remote(ag[p].at[3, 0], ag[p].at[2, 0], along(PART_AXES[p][2], 1)))
    for p in range(3):
        axis = PART_AXES[p][2]
        rest.append(remote(ag[p].at[0, pl.ds(2, 2)], ag[p].at[3, pl.ds(2, 2)], along(axis, 1)))
        rest.append(remote(ag[p].at[0, 1], ag[p].at[1, 1], along(axis, 3)))
    for i in range(2, 5):
        near_step(i)
    for p in range(3):
        axis = PART_AXES[p][2]
        third[3 * p].wait_recv()
        relay.append(remote(ag[p].at[3, 1], ag[p].at[2, 1], along(axis, 1)))
        third[3 * p + 1].wait_recv()
        relay.append(remote(ag[p].at[1, 2], ag[p].at[2, 2], along(axis, 3)))
    for p in range(3):
        third[3 * p + 2].wait_recv()
        relay.append(remote(ag[p].at[1, 3], ag[p].at[2, 3], along(PART_AXES[p][2], 3)))
    w_copy.wait_recv()

    def sibling_step(q, _):
        cols = pl.ds(pl.multiple_of(q * 512, 512), 512)
        upper, rest = split(w_sib[:, cols])
        wb[pl.ds(other, RANK), cols] = upper
        wb[pl.ds(128 + other, RANK), cols] = rest
        return 0

    lax.fori_loop(0, 16, sibling_step, 0)
    for i in range(16):
        wt[i * 512:(i + 1) * 512, :] = wb[:, i * 512:(i + 1) * 512].T
    for i in range(5, NCHUNK):
        near_step(i)
    for p in range(3):
        early[2 * p + 1].wait_recv()
    for copy in rest + relay:
        copy.wait_recv()

    def columns(ax, ay):
        q = (pos[0] + ax) % 4 * 16 + (pos[1] + ay) % 4 * 4
        return pl.ds(pl.multiple_of(q * 128, 512), 512)

    total = None
    for ax in range(4):
        for ay in range(4):
            blocks = []
            for qz in range(4):
                az = (qz + 4 - pos[2]) % 4
                blocks.append(jnp.concatenate([ag0[az, ay, ax], ag1[ax, az, ay], ag2[ay, ax, az]], axis=0))
            upper, rest = split(jnp.concatenate(blocks, axis=1))
            part = nn(jnp.concatenate([upper, rest], axis=0), wt[columns(ax, ay), :])
            total = part if total is None else total + part
    comb[...] = total[:HALF, :128] + (total[:HALF, 128:] + total[HALF:, :128])
    comb_copy = remote(comb, comb_in, sibling)
    obs_in.wait()
    read_in.wait()
    comb_copy.wait_recv()
    valid = lax.broadcasted_iota(jnp.int32, (HALF, RDEV), 1) < counts[0, 0]
    for rows, source in ((mine, comb), (other, comb_in)):
        far = nn(source[...].astype(BF16), rpad[...])
        value = jnp.where(valid, mis[pl.ds(rows, HALF), :] + far - obsv[pl.ds(rows, HALF), :], 0.0)
        mis[pl.ds(rows, HALF), :] = value
        rb[pl.ds(rows, HALF), :] = value.astype(BF16)
    tr[...] = nt(rb[...], rpad[...])
    used[0] = 0
    outs = [local(mv, mom_out), local(mis, mis_out)]
    tr_copy = remote(tr.at[pl.ds(other, HALF)], tr_in, sibling)

    lanes = lax.broadcasted_iota(jnp.int32, (MEMB, 128), 1)

    def edge_cols(array, start, stop, low, high):
        for r in range(start, stop):
            value = array[:, r * 128:(r + 1) * 128].astype(F32)
            turned = pltpu.roll(value, r, 1) if r else value
            low = jnp.where(lanes == r, turned, low)
            high = jnp.where(lanes == (r + 127) % 128, turned, high)
        return low, high

    blank = jnp.zeros((MEMB, 128), F32)

    def grad_step(i):
        grad[:, i * NROWS:(i + 1) * NROWS] = nt(rb[...], nearv[i * NROWS:(i + 1) * NROWS, :])

    grid_row = lat * 16 + lax.broadcasted_iota(jnp.int32, (16, 128), 0)
    spacing = 2.0 * lat_limit / 128
    latitude = -lat_limit + (grid_row.astype(F32) + 0.5) * spacing
    centre = jnp.cos(latitude)
    c_lon = 0.25 / (centre * centre)
    c_north = 0.25 * jnp.cos(latitude + 0.5 * spacing) / centre
    c_south = 0.25 * jnp.cos(latitude - 0.5 * spacing) / centre
    scale = step_size / (1.0 + c_north + c_south + 2.0 * c_lon)
    coef[0] = scale
    coef[1] = jnp.where(grid_row < 127, scale * c_north, 0.0)
    coef[2] = jnp.where(grid_row > 0, scale * c_south, 0.0)
    coef[3] = scale * c_lon
    outs.append(local(coef, coef_out))
    low, high = edge_cols(dpad, 0, ROWS, blank, blank)
    base_w[...] = low.astype(BF16)
    base_e[...] = high.astype(BF16)
    tr_copy.wait_recv()
    pair = (tr[pl.ds(mine, HALF), :] + tr_in[...]).astype(BF16)
    pair = jnp.concatenate([pair, pair], axis=1)

    def partial_step(ax, ay):
        for half in range(2):
            q = (pos[0] + ax) % 4 * 16 + (pos[1] + ay) % 4 * 4 + 2 * half
            value = nn(pair, wb[:, pl.ds(pl.multiple_of(q * 128, 256), 256)])
            for qz in range(2):
                az = (2 * half + qz + 4 - pos[2]) % 4
                piece = value[:, qz * 128:(qz + 1) * 128]
                rs0[az, ay, ax] = piece[PART_START[0]:PART_START[1]]
                rs1[ax, az, ay] = piece[PART_START[1]:PART_START[2]]
                rs2[ay, ax, az] = piece[PART_START[2]:]

    used[1] = 0
    opp = {}

    def send_opposite(p):
        axis = PART_AXES[p][2]
        opp[p, 1] = remote(rs[p].at[2, 1], rin[p].at[0], along(axis, 1))
        opp[p, 2] = remote(rs[p].at[2, 2], rin[p].at[1], along(axis, 3))
        opp[p, 3] = remote(rs[p].at[2, 3], rin[p].at[2], along(axis, 3))

    for ay in range(4):
        partial_step(2, ay)
    send_opposite(1)
    for ax in (0, 1, 3):
        partial_step(ax, 2)
    send_opposite(2)
    for ax in (0, 1, 3):
        for ay in (0, 1, 3):
            partial_step(ax, ay)
    send_opposite(0)
    direct = []
    for p in (1, 2, 0):
        axis = PART_AXES[p][2]
        direct.append(remote(rs[p].at[1, pl.ds(2, 2)], rin[p].at[pl.ds(4, 2)], along(axis, 1)))
        direct.append(remote(rs[p].at[3, 1], rin[p].at[3], along(axis, 3)))
        opp[p, 0] = remote(rs[p].at[2, 0], rin[p].at[6], along(axis, 1))
    for i in range(0, 3):
        grad_step(i)
    dep, late = [], []
    for p in (1, 2, 0):
        axis = PART_AXES[p][2]
        opp[p, 1].wait_recv()
        rs[p][1, 1] = rs[p][1, 1] + rin[p][0]
        dep.append(remote(rs[p].at[1, 1], rin[p].at[7], along(axis, 1)))
        opp[p, 2].wait_recv()
        rs[p][3, 2] = rs[p][3, 2] + rin[p][1]
        dep.append(remote(rs[p].at[3, 2], rin[p].at[8], along(axis, 3)))
    for p in (1, 2, 0):
        opp[p, 3].wait_recv()
        rs[p][3, 3] = rs[p][3, 3] + rin[p][2]
        dep.append(remote(rs[p].at[3, 3], rin[p].at[9], along(PART_AXES[p][2], 3)))
    for p in (1, 2, 0):
        axis = PART_AXES[p][2]
        late.append(remote(rs[p].at[3, 0], rin[p].at[10], along(axis, 3)))
        opp[p, 0].wait_recv()
        rs[p][1, 0] = rs[p][1, 0] + rin[p][6]
        late.append(remote(rs[p].at[1, 0], rin[p].at[11], along(axis, 1)))
    for i in range(3, 10):
        grad_step(i)
    for copy in direct + dep:
        copy.wait_recv()
    near_owner = []
    for p in range(3):
        rs[p][0, 2] = rs[p][0, 2] + rin[p][4] + rin[p][8]
        near_owner.append(remote(rs[p].at[0, 2], two[p].at[1], along(PART_AXES[p][1], 2)))
    for p in range(3):
        rs[p][0, 1] = rs[p][0, 1] + rin[p][3] + rin[p][7]
        near_owner.append(remote(rs[p].at[0, 1], two[p].at[0], along(PART_AXES[p][1], 1)))
        rs[p][0, 3] = rs[p][0, 3] + rin[p][5] + rin[p][9]
        near_owner.append(remote(rs[p].at[0, 3], two[p].at[2], along(PART_AXES[p][1], 3)))
    for i in range(10, NCHUNK):
        grad_step(i)
    for copy in late:
        copy.wait_recv()
    for p in range(3):
        rs[p][0, 0] = rs[p][0, 0] + rin[p][10] + rin[p][11]
    for copy in near_owner:
        copy.wait_recv()
    last = []
    for p in range(3):
        rs[p][0, 0] = rs[p][0, 0] + two[p][0] + two[p][1] + two[p][2]
    for step in (2, 1, 3):
        for p in range(3):
            for on, place in ((core, one[p]), (1 - core, far_one[p])):
                last.append(remote(rs[p].at[0, 0, step], place.at[step - 1], along(PART_AXES[p][0], step, on)))
    for p in range(3):
        last.append(remote(rs[p].at[0, 0, 0], far_one[p].at[3], sibling))
    low, high = edge_cols(grad, 0, ROWS, blank, blank)
    edge_w[...] = low
    edge_e[...] = high
    for copy in last:
        copy.wait_recv()
    for p in range(3):
        for rows, value in (
            (mine, rs[p][0, 0, 0] + one[p][0] + one[p][1] + one[p][2]),
            (other, far_one[p][0] + far_one[p][1] + far_one[p][2] + far_one[p][3]),
        ):
            own[pl.ds(pl.multiple_of(rows + PART_START[p], 8), PART_ROWS[p]), :] = value
    owner = own[...].astype(BF16)

    def far_grad(start, width):
        cols = pl.ds(start, width)
        grad[:, cols] = grad[:, cols] + nn(owner, dpad[:, cols])

    edge_w[...] = edge_w[...] + nn(owner, base_w[...])
    edge_e[...] = edge_e[...] + nn(owner, base_e[...])
    borders = [remote(edge_w, he, west), remote(edge_e, hw, east)]
    for layer in range(3):
        cols = pl.ds(layer * 128, 128)
        start = layer * 2048
        far_grad(start, 128)
        borders.append(remote(grad.at[:, pl.ds(start, 128)], hn.at[:, cols], south))
        far_grad(start + 15 * 128, 128)
        borders.append(remote(grad.at[:, pl.ds(start + 15 * 128, 128)], hs.at[:, cols], north))
    for layer in range(3):
        for start in range(128, 1920, 256):
            far_grad(layer * 2048 + start, 256)
        cols = pl.ds(layer * 2048, 2048)
        outs.append(local(grad.at[:, cols], grad_out.at[:, cols]))
    for copy in borders:
        copy.wait_recv()
    halo[:, 0:384] = hn[...]
    halo[:, 384:768] = hs[...]
    from_west = pltpu.roll(hw[...], 2, 1)
    halo[:, 768:896] = jnp.where(lanes % 2 == 0, he[...], from_west)
    halo[:, 896:1024] = jnp.where(lanes % 2 == 1, he[...], from_west)
    outs.append(local(halo, halo_out))
    for copy in sent[-SENDS:]:
        copy.wait_send()
    assert used[2] <= RECVS
    for copy in outs:
        copy.wait()


def smooth_kernel(mom, grad, mis, halo, coef, out, mis_out):
    members = mis_out.shape[0]
    mis_out[...] = mis[...]
    lanes = lax.broadcasted_iota(jnp.int32, (members, 128), 1)
    edges = (halo[:, 768:896], halo[:, 896:1024])
    for r in range(ROWS):
        layer, row = r // 16, r % 16
        here = grad[:, r * 128:(r + 1) * 128]
        above = (
            halo[:, layer * 128:(layer + 1) * 128] if row == 15 else grad[:, (r + 1) * 128:(r + 2) * 128]
        )
        below = (
            halo[:, 384 + layer * 128:384 + (layer + 1) * 128] if row == 0 else grad[:, (r - 1) * 128:r * 128]
        )
        edge = pltpu.roll(edges[r % 2], 127 - r, 1)
        right = jnp.where(lanes == 127, edge, pltpu.roll(here, 127, 1))
        left = jnp.where(lanes == 0, edge, pltpu.roll(here, 1, 1))
        change = (
            coef[0, row:row + 1, :] * here
            + coef[1, row:row + 1, :] * above
            + coef[2, row:row + 1, :] * below
            + coef[3, row:row + 1, :] * (right + left)
        )
        out[pl.ds(r, members, stride=ROWS), :] = mom[pl.ds(r, members, stride=ROWS), :] - change


def shards(moments, observed, counts, near_kernel, dipole_basis, reading_basis, coupling, ranks):
    mom = moments.reshape(MEMB * ROWS, 128)
    hbm = pl.BlockSpec(memory_space=pl.ANY)
    smem = pl.BlockSpec(memory_space=pltpu.SMEM)
    vmem = pltpu.VMEM
    parts = PART_ROWS
    grad, loaded, misfit, halo, coef = pl.pallas_call(
        exchange_kernel,
        out_shape=[
            vmem((MEMB, ND), F32),
            vmem((MEMB * ROWS, 128), F32),
            vmem((MEMB, RDEV), F32),
            vmem((MEMB, 1024), F32),
            vmem((4, 16, 128), F32),
        ],
        in_specs=[hbm, hbm, smem, hbm, hbm, hbm, hbm, smem],
        out_specs=[hbm] * 5,
        scratch_shapes=[
            vmem((MEMB, ND), F32),
            vmem((MEMB * ROWS, 128), F32),
            vmem((MEMB, RDEV), F32),
            vmem((MEMB, 1024), F32),
            vmem((4, 16, 128), F32),
            vmem((WIDE, 256), BF16),
            vmem((MEMB, ND), BF16),
            vmem((ND, RDEV), BF16),
            vmem((128, ND), BF16),
            vmem((128, RDEV), BF16),
            vmem((MEMB, RDEV), F32),
            vmem((RANK, WIDE), F32),
            vmem((RANK, WIDE), F32),
            vmem((256, WIDE), BF16),
            vmem((MEMB, RDEV), BF16),
            vmem((MEMB, 128), F32),
            vmem((HALF, 128), F32),
            vmem((HALF, 128), F32),
            vmem((HALF, 128), F32),
            vmem((MEMB, 128), F32),
            vmem((HALF, 128), F32),
            vmem((MEMB, 128), F32),
            vmem((MEMB, 128), F32),
            vmem((MEMB, 128), F32),
            vmem((128, 128), BF16),
            vmem((128, 128), BF16),
            vmem((MEMB, 384), F32),
            vmem((MEMB, 384), F32),
            vmem((MEMB, 128), F32),
            vmem((MEMB, 128), F32),
        ]
        + [vmem((4, 4, 4, n, 128), F32) for n in parts]
        + [vmem((4, 4, 4, n, 128), F32) for n in parts]
        + [vmem((12, 4, n, 128), F32) for n in parts]
        + [vmem((3, 4, n, 128), F32) for n in parts]
        + [vmem((3, n, 128), F32) for n in parts]
        + [vmem((4, n, 128), F32) for n in parts]
        + [vmem((3, n, 128), F32) for n in parts] * 2
        + [pltpu.SemaphoreType.DMA((SENDS,)), pltpu.SemaphoreType.DMA((RECVS,)), pltpu.SemaphoreType.DMA((16,))],
        compiler_params=pltpu.CompilerParams(
            collective_id=0, has_side_effects=True, vmem_limit_bytes=48 * 1024 * 1024
        ),
        cost_estimate=pl.CostEstimate(flops=3_700_000_000, bytes_accessed=24_000_000, transcendentals=0),
        name="exchange",
    )(
        mom, observed[0, 0], counts, near_kernel[0, 0], dipole_basis[0, 0].T, reading_basis[0, 0].T,
        coupling[0, 0], ranks[0],
    )
    members = 16
    new, misfit = pl.pallas_call(
        smooth_kernel,
        grid=(MEMB // members,),
        out_shape=[
            jax.ShapeDtypeStruct((MEMB * ROWS, 128), F32),
            jax.ShapeDtypeStruct((MEMB, RDEV), F32),
        ],
        in_specs=[
            pl.BlockSpec((members * ROWS, 128), lambda i: (i, 0)),
            pl.BlockSpec((members, ND), lambda i: (i, 0)),
            pl.BlockSpec((members, RDEV), lambda i: (i, 0)),
            pl.BlockSpec((members, 1024), lambda i: (i, 0)),
            pl.BlockSpec((4, 16, 128), lambda i: (0, 0, 0)),
        ],
        out_specs=[
            pl.BlockSpec((members * ROWS, 128), lambda i: (i, 0)),
            pl.BlockSpec((members, RDEV), lambda i: (i, 0)),
        ],
        compiler_params=pltpu.CompilerParams(vmem_limit_bytes=32 * 1024 * 1024),
        cost_estimate=pl.CostEstimate(flops=10_000_000, bytes_accessed=4_000_000, transcendentals=0),
        name="smooth",
    )(loaded, grad, misfit, halo, coef)
    return new.reshape(moments.shape), misfit[None, None]


def solution(mesh):
    return jax.shard_map(
        shards,
        mesh=mesh,
        in_specs=(
            P(None, None, "lat", "lon"),
            P("lat", "lon", None, None),
            P("lat", "lon"),
            P("lat", "lon", None, None),
            P("lat", "lon", None, None),
            P("lat", "lon", None, None),
            P("lat", "lon", None, None),
            P("lat", "lon", None),
        ),
        out_specs=(P(None, None, "lat", "lon"), P("lat", "lon", None, None)),
        check_vma=False,
    )
```

```python
import functools

import jax
import jax.numpy as jnp
from jax import lax
from jax.experimental import pallas as pl
from jax.experimental.pallas import tpu as pltpu
from jax.sharding import PartitionSpec as P

step_size = 0.5
lat_limit = 1.25
MESH = pl.DeviceIdType.MESH
F32 = jnp.float32
BF16 = jnp.bfloat16

MEMB = 128
HALF = 64
ROWS = 48
ND = 6144
RDEV = 1024
RANK = 64
WIDE = 8192
PART_ROWS = (16, 24, 24)
PART_START = (0, 16, 40)
PART_AXES = ((0, 1, 2), (1, 2, 0), (2, 0, 1))
MCHUNK = 8
SENDS = 32
RECVS = 73
NCHUNK = 12
NROWS = ND // NCHUNK


def nt(a, b):
    return lax.dot_general(a, b, (((1,), (1,)), ((), ())), preferred_element_type=F32)


def nn(a, b):
    return jnp.dot(a, b, preferred_element_type=F32)


def exchange_kernel(
    mom, obs, counts, near, dip_t, read_t, coup, ranks,
    grad_out, mom_out, mis_out, halo_out, coef_out,
    grad, mv, mis, halo, coef, wt,
    mbits, nearv, dpad, rpad, obsv, w_own, w_sib, wb, rb, sk, sk_in, comb, comb_in,
    read_out, read_in_f32, rsib, dif, dif_in, own, edge_w, edge_e, base_w, base_e, hn, hs, he, hw,
    ag0, ag1, ag2, rs0, rs1, rs2, in0, in1, in2, two0, two1, two2, one0, one1, one2,
    far0, far1, far2, same0, same1, same2, cross0, cross1, cross2,
    ssem, rsem, lsem,
):
    ag, rs, rin = (ag0, ag1, ag2), (rs0, rs1, rs2), (in0, in1, in2)
    two, one, far_one = (two0, two1, two2), (one0, one1, one2), (far0, far1, far2)
    same, cross = (same0, same1, same2), (cross0, cross1, cross2)
    lon = lax.axis_index("lon")
    lat = lax.axis_index("lat")
    pos = (lon // 4, lon % 4, lat // 2)
    core = lat % 2
    mine = pl.multiple_of(core * HALF, HALF)
    other = pl.multiple_of((1 - core) * HALF, HALF)

    def along(axis, step, on=core):
        p = list(pos)
        p[axis] = (p[axis] + step) % 4
        return (p[0] * 4 + p[1], p[2] * 2 + on)

    sibling = (lon, pos[2] * 2 + 1 - core)
    north, south = (lon, (lat + 1) % 8), (lon, (lat + 7) % 8)
    east, west = ((lon + 1) % 16, lat), ((lon + 15) % 16, lat)

    peers = [sibling, north, south, east, west]
    peers += [along(axis, step, on) for axis in range(3) for step in (1, 2, 3) for on in (core, 1 - core)]
    barrier = pltpu.get_barrier_semaphore()
    for peer in peers:
        pl.semaphore_signal(barrier, inc=1, device_id=peer, device_id_type=MESH)

    used = [0, 0, 0]
    sent = []

    def local(src, dst):
        copy = pltpu.make_async_copy(src, dst, lsem.at[used[0]])
        used[0] += 1
        copy.start()
        return copy

    def remote(src, dst, peer):
        if len(sent) >= SENDS:
            sent[-SENDS].wait_send()
        copy = pltpu.make_async_remote_copy(
            src_ref=src, dst_ref=dst, send_sem=ssem.at[len(sent) % SENDS], recv_sem=rsem.at[used[1]],
            device_id=peer, device_id_type=MESH,
        )
        used[1] += 1
        used[2] = max(used[2], used[1])
        copy.start()
        sent.append(copy)
        return copy

    msize = ND // MCHUNK
    mom_in = [local(mom.at[pl.ds(i * msize, msize)], mv.at[pl.ds(i * msize, msize)]) for i in range(MCHUNK)]
    used[0] = 12
    dip_in = local(dip_t, dpad.at[pl.ds(mine, RANK)])
    coup_in = local(coup, w_own)
    read_in = local(read_t, rpad.at[pl.ds(mine, RANK)])
    obs_in = local(obs, obsv)
    dpad[pl.ds(other, RANK), :] = jnp.zeros((RANK, ND), BF16)
    rpad[pl.ds(other, RANK), :] = jnp.zeros((RANK, RDEV), BF16)
    members = MEMB // MCHUNK

    for i in range(MCHUNK):
        mom_in[i].wait()
        for r in range(ROWS):
            mbits[i * members:(i + 1) * members, r * 128:(r + 1) * 128] = mv[
                pl.ds(i * msize + r, members, stride=ROWS), :
            ].astype(BF16)
    dip_in.wait()
    sk[...] = nt(mbits[...], dpad[...])
    pl.semaphore_wait(barrier, len(peers))

    sk_copy = remote(sk.at[pl.ds(other, HALF)], sk_in, sibling)
    first = []
    for step in (2, 1, 3):
        for p in range(3):
            for on, rows, place in ((core, mine, same[p]), (1 - core, other, cross[p])):
                source = sk.at[pl.ds(pl.multiple_of(rows + PART_START[p], 8), PART_ROWS[p])]
                first.append(remote(source, place.at[step - 1], along(PART_AXES[p][0], step, on)))
    used[0] = 0
    near_in = [
        local(near.at[pl.ds(i * NROWS, NROWS)], nearv.at[pl.ds(i * NROWS, NROWS)]) for i in range(NCHUNK)
    ]

    coup_in.wait()
    lane = lax.broadcasted_iota(jnp.int32, (RANK, 128), 1)
    row = lax.broadcasted_iota(jnp.int32, (RANK, 128), 0)
    inner = jnp.maximum(row, lane % RANK)

    def split(value):
        upper = value.astype(BF16)
        return upper, (value - upper.astype(F32)).astype(BF16)

    def mask_step(q, _):
        cols = pl.ds(pl.multiple_of(q * 128, 128), 128)
        limit = jnp.where(lane < RANK, ranks[0, 2 * q], ranks[0, 2 * q + 1])
        value = jnp.where(inner < limit, w_own[:, cols], 0.0)
        w_own[:, cols] = value
        upper, rest = split(value)
        wb[pl.ds(mine, RANK), cols] = upper
        wb[pl.ds(128 + mine, RANK), cols] = rest
        return 0

    lax.fori_loop(0, 24, mask_step, 0)

    def near_step(i):
        near_in[i].wait()
        part = nn(mbits[:, i * NROWS:(i + 1) * NROWS], nearv[i * NROWS:(i + 1) * NROWS, :])
        if i == 0:
            mis[...] = part
        else:
            mis[...] += part

    sk_copy.wait_recv()
    block = sk[pl.ds(mine, HALF), :] + sk_in[...]
    for p in range(3):
        ag[p][0, 0, 0] = block[PART_START[p]:PART_START[p] + PART_ROWS[p]]
    for copy in first:
        copy.wait_recv()
    for p in range(3):
        for step in (1, 2, 3):
            ag[p][0, 0, 4 - step] = same[p][step - 1] + cross[p][step - 1]
    second = []
    for step in (2, 1, 3):
        for p in range(3):
            second.append(remote(ag[p].at[0, 0], ag[p].at[0, 4 - step], along(PART_AXES[p][1], step)))
    early = []
    for p in range(3):
        axis = PART_AXES[p][2]
        early.append(remote(ag[p].at[0, 0], ag[p].at[3, 0], along(axis, 1)))
        early.append(remote(ag[p].at[0, 0], ag[p].at[1, 0], along(axis, 3)))
    lax.fori_loop(24, 64, mask_step, 0)
    w_copy = remote(w_own, w_sib, sibling)
    read_in.wait()
    valid = lax.broadcasted_iota(jnp.int32, (HALF, RDEV), 1) < counts[0, 0]
    read_out[...] = jnp.where(valid, rpad[pl.ds(mine, RANK), :].astype(F32), 0.0)
    read_copy = remote(read_out, read_in_f32, sibling)
    for i in range(0, 2):
        near_step(i)
    for copy in second:
        copy.wait_recv()
    third, relay, rest = [], [], []
    for p in range(3):
        axis = PART_AXES[p][2]
        third.append(remote(ag[p].at[0, 1], ag[p].at[3, 1], along(axis, 1)))
        third.append(remote(ag[p].at[0, 2], ag[p].at[1, 2], along(axis, 3)))
        third.append(remote(ag[p].at[0, 3], ag[p].at[1, 3], along(axis, 3)))
    for p in range(3):
        early[2 * p].wait_recv()
        relay.append(remote(ag[p].at[3, 0], ag[p].at[2, 0], along(PART_AXES[p][2], 1)))
    for p in range(3):
        axis = PART_AXES[p][2]
        rest.append(remote(ag[p].at[0, pl.ds(2, 2)], ag[p].at[3, pl.ds(2, 2)], along(axis, 1)))
        rest.append(remote(ag[p].at[0, 1], ag[p].at[1, 1], along(axis, 3)))
    for i in range(2, 5):
        near_step(i)
    for p in range(3):
        axis = PART_AXES[p][2]
        third[3 * p].wait_recv()
        relay.append(remote(ag[p].at[3, 1], ag[p].at[2, 1], along(axis, 1)))
        third[3 * p + 1].wait_recv()
        relay.append(remote(ag[p].at[1, 2], ag[p].at[2, 2], along(axis, 3)))
    for p in range(3):
        third[3 * p + 2].wait_recv()
        relay.append(remote(ag[p].at[1, 3], ag[p].at[2, 3], along(PART_AXES[p][2], 3)))
    w_copy.wait_recv()

    def sibling_step(q, _):
        cols = pl.ds(pl.multiple_of(q * 512, 512), 512)
        upper, rest = split(w_sib[:, cols])
        wb[pl.ds(other, RANK), cols] = upper
        wb[pl.ds(128 + other, RANK), cols] = rest
        return 0

    lax.fori_loop(0, 16, sibling_step, 0)
    for i in range(16):
        wt[i * 512:(i + 1) * 512, :] = wb[:, i * 512:(i + 1) * 512].T
    for i in range(5, NCHUNK):
        near_step(i)
    obs_in.wait()
    mis[...] = mis[...] - obsv[...]
    dif[...] = mis[pl.ds(other, HALF), :]
    dif_copy = remote(dif, dif_in, sibling)
    read_copy.wait_recv()
    rsib[pl.ds(other, RANK), :] = read_in_f32[...].astype(BF16)
    rsib[pl.ds(mine, RANK), :] = jnp.zeros((RANK, RDEV), BF16)
    for p in range(3):
        early[2 * p + 1].wait_recv()
    for copy in rest + relay:
        copy.wait_recv()

    def columns(ax, ay):
        q = (pos[0] + ax) % 4 * 16 + (pos[1] + ay) % 4 * 4
        return pl.ds(pl.multiple_of(q * 128, 512), 512)

    total = None
    for ax in range(4):
        for ay in range(4):
            blocks = []
            for qz in range(4):
                az = (qz + 4 - pos[2]) % 4
                blocks.append(jnp.concatenate([ag0[az, ay, ax], ag1[ax, az, ay], ag2[ay, ax, az]], axis=0))
            upper, rest = split(jnp.concatenate(blocks, axis=1))
            part = nn(jnp.concatenate([upper, rest], axis=0), wt[columns(ax, ay), :])
            total = part if total is None else total + part
    comb[...] = total[:HALF, :128] + (total[:HALF, 128:] + total[HALF:, :128])
    comb_copy = remote(comb, comb_in, sibling)

    def residual(rows, source):
        value = jnp.where(valid, mis[pl.ds(rows, HALF), :] + nn(source[...].astype(BF16), rpad[...]), 0.0)
        mis[pl.ds(rows, HALF), :] = value
        value = value.astype(BF16)
        rb[pl.ds(rows, HALF), :] = value
        return value

    dif_copy.wait_recv()
    here = residual(mine, comb)
    there = (dif_in[...] + nn(comb[...].astype(BF16), rsib[...])).astype(BF16)
    pair = (nt(here, rpad[...]) + nt(there, rsib[...])).astype(BF16)
    pair = jnp.concatenate([pair, pair], axis=1)
    lanes = lax.broadcasted_iota(jnp.int32, (MEMB, 128), 1)

    def edge_cols(array, start, stop, low, high):
        for r in range(start, stop):
            value = array[:, r * 128:(r + 1) * 128].astype(F32)
            turned = pltpu.roll(value, r, 1) if r else value
            low = jnp.where(lanes == r, turned, low)
            high = jnp.where(lanes == (r + 127) % 128, turned, high)
        return low, high

    blank = jnp.zeros((MEMB, 128), F32)

    def grad_step(i):
        grad[:, i * NROWS:(i + 1) * NROWS] = nt(rb[...], nearv[i * NROWS:(i + 1) * NROWS, :])

    def partial_step(ax, ay):
        for half in range(2):
            q = (pos[0] + ax) % 4 * 16 + (pos[1] + ay) % 4 * 4 + 2 * half
            value = nn(pair, wb[:, pl.ds(pl.multiple_of(q * 128, 256), 256)])
            for qz in range(2):
                az = (2 * half + qz + 4 - pos[2]) % 4
                piece = value[:, qz * 128:(qz + 1) * 128]
                rs0[az, ay, ax] = piece[PART_START[0]:PART_START[1]]
                rs1[ax, az, ay] = piece[PART_START[1]:PART_START[2]]
                rs2[ay, ax, az] = piece[PART_START[2]:]

    used[1] = 0
    opp = {}

    def send_opposite(p):
        axis = PART_AXES[p][2]
        opp[p, 1] = remote(rs[p].at[2, 1], rin[p].at[0], along(axis, 1))
        opp[p, 2] = remote(rs[p].at[2, 2], rin[p].at[1], along(axis, 3))
        opp[p, 3] = remote(rs[p].at[2, 3], rin[p].at[2], along(axis, 3))

    for ay in range(4):
        partial_step(2, ay)
    send_opposite(1)
    for ax in (0, 1, 3):
        partial_step(ax, 2)
    send_opposite(2)
    for ax in (0, 1, 3):
        for ay in (0, 1, 3):
            partial_step(ax, ay)
    send_opposite(0)
    direct = []
    for p in (1, 2, 0):
        axis = PART_AXES[p][2]
        direct.append(remote(rs[p].at[1, pl.ds(2, 2)], rin[p].at[pl.ds(4, 2)], along(axis, 1)))
        direct.append(remote(rs[p].at[3, 1], rin[p].at[3], along(axis, 3)))
        opp[p, 0] = remote(rs[p].at[2, 0], rin[p].at[6], along(axis, 1))
    comb_copy.wait_recv()
    residual(other, comb_in)
    used[0] = 0
    outs = [local(mv, mom_out), local(mis, mis_out)]
    grid_row = lat * 16 + lax.broadcasted_iota(jnp.int32, (16, 128), 0)
    spacing = 2.0 * lat_limit / 128
    latitude = -lat_limit + (grid_row.astype(F32) + 0.5) * spacing
    centre = jnp.cos(latitude)
    c_lon = 0.25 / (centre * centre)
    c_north = 0.25 * jnp.cos(latitude + 0.5 * spacing) / centre
    c_south = 0.25 * jnp.cos(latitude - 0.5 * spacing) / centre
    scale = step_size / (1.0 + c_north + c_south + 2.0 * c_lon)
    coef[0] = scale
    coef[1] = jnp.where(grid_row < 127, scale * c_north, 0.0)
    coef[2] = jnp.where(grid_row > 0, scale * c_south, 0.0)
    coef[3] = scale * c_lon
    outs.append(local(coef, coef_out))
    low, high = edge_cols(dpad, 0, ROWS, blank, blank)
    base_w[...] = low.astype(BF16)
    base_e[...] = high.astype(BF16)
    for i in range(0, 2):
        grad_step(i)
    dep, late = [], []
    for p in (1, 2, 0):
        axis = PART_AXES[p][2]
        opp[p, 1].wait_recv()
        rs[p][1, 1] = rs[p][1, 1] + rin[p][0]
        dep.append(remote(rs[p].at[1, 1], rin[p].at[7], along(axis, 1)))
        opp[p, 2].wait_recv()
        rs[p][3, 2] = rs[p][3, 2] + rin[p][1]
        dep.append(remote(rs[p].at[3, 2], rin[p].at[8], along(axis, 3)))
    for p in (1, 2, 0):
        opp[p, 3].wait_recv()
        rs[p][3, 3] = rs[p][3, 3] + rin[p][2]
        dep.append(remote(rs[p].at[3, 3], rin[p].at[9], along(PART_AXES[p][2], 3)))
    for p in (1, 2, 0):
        axis = PART_AXES[p][2]
        late.append(remote(rs[p].at[3, 0], rin[p].at[10], along(axis, 3)))
        opp[p, 0].wait_recv()
        rs[p][1, 0] = rs[p][1, 0] + rin[p][6]
        late.append(remote(rs[p].at[1, 0], rin[p].at[11], along(axis, 1)))
    for i in range(2, 10):
        grad_step(i)
    for copy in direct + dep:
        copy.wait_recv()
    near_owner = []
    for p in range(3):
        rs[p][0, 2] = rs[p][0, 2] + rin[p][4] + rin[p][8]
        near_owner.append(remote(rs[p].at[0, 2], two[p].at[1], along(PART_AXES[p][1], 2)))
    for p in range(3):
        rs[p][0, 1] = rs[p][0, 1] + rin[p][3] + rin[p][7]
        near_owner.append(remote(rs[p].at[0, 1], two[p].at[0], along(PART_AXES[p][1], 1)))
        rs[p][0, 3] = rs[p][0, 3] + rin[p][5] + rin[p][9]
        near_owner.append(remote(rs[p].at[0, 3], two[p].at[2], along(PART_AXES[p][1], 3)))
    for i in range(10, NCHUNK):
        grad_step(i)
    for copy in late:
        copy.wait_recv()
    for p in range(3):
        rs[p][0, 0] = rs[p][0, 0] + rin[p][10] + rin[p][11]
    for copy in near_owner:
        copy.wait_recv()
    last = []
    for p in range(3):
        rs[p][0, 0] = rs[p][0, 0] + two[p][0] + two[p][1] + two[p][2]
    for step in (2, 1, 3):
        for p in range(3):
            for on, place in ((core, one[p]), (1 - core, far_one[p])):
                last.append(remote(rs[p].at[0, 0, step], place.at[step - 1], along(PART_AXES[p][0], step, on)))
    for p in range(3):
        last.append(remote(rs[p].at[0, 0, 0], far_one[p].at[3], sibling))
    low, high = edge_cols(grad, 0, ROWS, blank, blank)
    edge_w[...] = low
    edge_e[...] = high
    for copy in last:
        copy.wait_recv()
    for p in range(3):
        for rows, value in (
            (mine, rs[p][0, 0, 0] + one[p][0] + one[p][1] + one[p][2]),
            (other, far_one[p][0] + far_one[p][1] + far_one[p][2] + far_one[p][3]),
        ):
            own[pl.ds(pl.multiple_of(rows + PART_START[p], 8), PART_ROWS[p]), :] = value
    owner = own[...].astype(BF16)

    def far_grad(start, width):
        cols = pl.ds(start, width)
        grad[:, cols] = grad[:, cols] + nn(owner, dpad[:, cols])

    edge_w[...] = edge_w[...] + nn(owner, base_w[...])
    edge_e[...] = edge_e[...] + nn(owner, base_e[...])
    borders = [remote(edge_w, he, west), remote(edge_e, hw, east)]
    for layer in range(3):
        cols = pl.ds(layer * 128, 128)
        start = layer * 2048
        far_grad(start, 128)
        borders.append(remote(grad.at[:, pl.ds(start, 128)], hn.at[:, cols], south))
        far_grad(start + 15 * 128, 128)
        borders.append(remote(grad.at[:, pl.ds(start + 15 * 128, 128)], hs.at[:, cols], north))
    for layer in range(3):
        for start in range(128, 1920, 256):
            far_grad(layer * 2048 + start, 256)
        cols = pl.ds(layer * 2048, 2048)
        outs.append(local(grad.at[:, cols], grad_out.at[:, cols]))
    for copy in borders:
        copy.wait_recv()
    halo[:, 0:384] = hn[...]
    halo[:, 384:768] = hs[...]
    from_west = pltpu.roll(hw[...], 2, 1)
    halo[:, 768:896] = jnp.where(lanes % 2 == 0, he[...], from_west)
    halo[:, 896:1024] = jnp.where(lanes % 2 == 1, he[...], from_west)
    outs.append(local(halo, halo_out))
    for copy in sent[-SENDS:]:
        copy.wait_send()
    assert used[2] <= RECVS
    for copy in outs:
        copy.wait()


def smooth_kernel(mom, grad, mis, halo, coef, out, mis_out):
    members = mis_out.shape[0]
    mis_out[...] = mis[...]
    lanes = lax.broadcasted_iota(jnp.int32, (members, 128), 1)
    edges = (halo[:, 768:896], halo[:, 896:1024])
    for r in range(ROWS):
        layer, row = r // 16, r % 16
        if row == 0:
            below = halo[:, 384 + layer * 128:384 + (layer + 1) * 128]
            here = grad[:, r * 128:(r + 1) * 128]
        if row == 15:
            above = halo[:, layer * 128:(layer + 1) * 128]
        else:
            above = grad[:, (r + 1) * 128:(r + 2) * 128]
        edge = pltpu.roll(edges[r % 2], 127 - r, 1)
        right = jnp.where(lanes == 127, edge, pltpu.roll(here, 127, 1))
        left = jnp.where(lanes == 0, edge, pltpu.roll(here, 1, 1))
        change = (
            coef[0, row:row + 1, :] * here
            + coef[1, row:row + 1, :] * above
            + coef[2, row:row + 1, :] * below
            + coef[3, row:row + 1, :] * (right + left)
        )
        out[pl.ds(r, members, stride=ROWS), :] = mom[pl.ds(r, members, stride=ROWS), :] - change
        below, here = here, above


def shards(moments, observed, counts, near_kernel, dipole_basis, reading_basis, coupling, ranks):
    mom = moments.reshape(MEMB * ROWS, 128)
    hbm = pl.BlockSpec(memory_space=pl.ANY)
    smem = pl.BlockSpec(memory_space=pltpu.SMEM)
    vmem = pltpu.VMEM
    parts = PART_ROWS
    grad, loaded, misfit, halo, coef = pl.pallas_call(
        exchange_kernel,
        out_shape=[
            vmem((MEMB, ND), F32),
            vmem((MEMB * ROWS, 128), F32),
            vmem((MEMB, RDEV), F32),
            vmem((MEMB, 1024), F32),
            vmem((4, 16, 128), F32),
        ],
        in_specs=[hbm, hbm, smem, hbm, hbm, hbm, hbm, smem],
        out_specs=[hbm] * 5,
        scratch_shapes=[
            vmem((MEMB, ND), F32),
            vmem((MEMB * ROWS, 128), F32),
            vmem((MEMB, RDEV), F32),
            vmem((MEMB, 1024), F32),
            vmem((4, 16, 128), F32),
            vmem((WIDE, 256), BF16),
            vmem((MEMB, ND), BF16),
            vmem((ND, RDEV), BF16),
            vmem((128, ND), BF16),
            vmem((128, RDEV), BF16),
            vmem((MEMB, RDEV), F32),
            vmem((RANK, WIDE), F32),
            vmem((RANK, WIDE), F32),
            vmem((256, WIDE), BF16),
            vmem((MEMB, RDEV), BF16),
            vmem((MEMB, 128), F32),
            vmem((HALF, 128), F32),
            vmem((HALF, 128), F32),
            vmem((HALF, 128), F32),
            vmem((RANK, RDEV), F32),
            vmem((RANK, RDEV), F32),
            vmem((128, RDEV), BF16),
            vmem((HALF, RDEV), F32),
            vmem((HALF, RDEV), F32),
            vmem((MEMB, 128), F32),
            vmem((MEMB, 128), F32),
            vmem((MEMB, 128), F32),
            vmem((128, 128), BF16),
            vmem((128, 128), BF16),
            vmem((MEMB, 384), F32),
            vmem((MEMB, 384), F32),
            vmem((MEMB, 128), F32),
            vmem((MEMB, 128), F32),
        ]
        + [vmem((4, 4, 4, n, 128), F32) for n in parts]
        + [vmem((4, 4, 4, n, 128), F32) for n in parts]
        + [vmem((12, 4, n, 128), F32) for n in parts]
        + [vmem((3, 4, n, 128), F32) for n in parts]
        + [vmem((3, n, 128), F32) for n in parts]
        + [vmem((4, n, 128), F32) for n in parts]
        + [vmem((3, n, 128), F32) for n in parts] * 2
        + [pltpu.SemaphoreType.DMA((SENDS,)), pltpu.SemaphoreType.DMA((RECVS,)), pltpu.SemaphoreType.DMA((16,))],
        compiler_params=pltpu.CompilerParams(
            collective_id=0, has_side_effects=True, vmem_limit_bytes=48 * 1024 * 1024
        ),
        cost_estimate=pl.CostEstimate(flops=3_700_000_000, bytes_accessed=24_000_000, transcendentals=0),
        name="exchange",
    )(
        mom, observed[0, 0], counts, near_kernel[0, 0], dipole_basis[0, 0].T, reading_basis[0, 0].T,
        coupling[0, 0], ranks[0],
    )
    members = 32
    new, misfit = pl.pallas_call(
        smooth_kernel,
        grid=(MEMB // members,),
        out_shape=[
            jax.ShapeDtypeStruct((MEMB * ROWS, 128), F32),
            jax.ShapeDtypeStruct((MEMB, RDEV), F32),
        ],
        in_specs=[
            pl.BlockSpec((members * ROWS, 128), lambda i: (i, 0)),
            pl.BlockSpec((members, ND), lambda i: (i, 0)),
            pl.BlockSpec((members, RDEV), lambda i: (i, 0)),
            pl.BlockSpec((members, 1024), lambda i: (i, 0)),
            pl.BlockSpec((4, 16, 128), lambda i: (0, 0, 0)),
        ],
        out_specs=[
            pl.BlockSpec((members * ROWS, 128), lambda i: (i, 0)),
            pl.BlockSpec((members, RDEV), lambda i: (i, 0)),
        ],
        compiler_params=pltpu.CompilerParams(vmem_limit_bytes=32 * 1024 * 1024),
        cost_estimate=pl.CostEstimate(flops=10_000_000, bytes_accessed=4_000_000, transcendentals=0),
        name="smooth",
    )(loaded, grad, misfit, halo, coef)
    return new.reshape(moments.shape), misfit[None, None]


def solution(mesh):
    return jax.shard_map(
        shards,
        mesh=mesh,
        in_specs=(
            P(None, None, "lat", "lon"),
            P("lat", "lon", None, None),
            P("lat", "lon"),
            P("lat", "lon", None, None),
            P("lat", "lon", None, None),
            P("lat", "lon", None, None),
            P("lat", "lon", None, None),
            P("lat", "lon", None),
        ),
        out_specs=(P(None, None, "lat", "lon"), P("lat", "lon", None, None)),
        check_vma=False,
    )
```

```python
import functools

import jax
import jax.numpy as jnp
from jax import lax
from jax.experimental import pallas as pl
from jax.experimental.pallas import tpu as pltpu
from jax.sharding import PartitionSpec as P

step_size = 0.5
lat_limit = 1.25
MESH = pl.DeviceIdType.MESH
F32 = jnp.float32
BF16 = jnp.bfloat16

MEMB = 128
HALF = 64
ROWS = 48
ND = 6144
RDEV = 1024
RANK = 64
WIDE = 8192
PART_ROWS = (16, 24, 24)
PART_START = (0, 16, 40)
PART_AXES = ((0, 1, 2), (1, 2, 0), (2, 0, 1))
MCHUNK = 8
SENDS = 32
RECVS = 73
NCHUNK = 12
NROWS = ND // NCHUNK


def nt(a, b):
    return lax.dot_general(a, b, (((1,), (1,)), ((), ())), preferred_element_type=F32)


def nn(a, b):
    return jnp.dot(a, b, preferred_element_type=F32)


def exchange_kernel(
    mom, obs, counts, near, dip_t, read_t, coup, ranks,
    grad_out, mom_out, mis_out, halo_out, coef_out,
    grad, mv, mis, halo, coef, wt,
    mbits, nearv, dpad, rpad, obsv, w_own, w_sib, wb, rb, sk, sk_in, comb, comb_in,
    read_out, read_in_f32, rsib, dif, dif_in, own, edge_w, edge_e, base_w, base_e, hn, hs, he, hw,
    ag0, ag1, ag2, rs0, rs1, rs2, in0, in1, in2, two0, two1, two2, one0, one1, one2,
    far0, far1, far2, same0, same1, same2, cross0, cross1, cross2,
    ssem, rsem, lsem,
):
    ag, rs, rin = (ag0, ag1, ag2), (rs0, rs1, rs2), (in0, in1, in2)
    two, one, far_one = (two0, two1, two2), (one0, one1, one2), (far0, far1, far2)
    same, cross = (same0, same1, same2), (cross0, cross1, cross2)
    lon = lax.axis_index("lon")
    lat = lax.axis_index("lat")
    pos = (lon // 4, lon % 4, lat // 2)
    core = lat % 2
    mine = pl.multiple_of(core * HALF, HALF)
    other = pl.multiple_of((1 - core) * HALF, HALF)

    def along(axis, step, on=core):
        p = list(pos)
        p[axis] = (p[axis] + step) % 4
        return (p[0] * 4 + p[1], p[2] * 2 + on)

    sibling = (lon, pos[2] * 2 + 1 - core)
    north, south = (lon, (lat + 1) % 8), (lon, (lat + 7) % 8)
    east, west = ((lon + 1) % 16, lat), ((lon + 15) % 16, lat)

    peers = [sibling, north, south, east, west]
    peers += [along(axis, step, on) for axis in range(3) for step in (1, 2, 3) for on in (core, 1 - core)]
    barrier = pltpu.get_barrier_semaphore()

    used = [0, 0, 0]
    sent = []

    def local(src, dst):
        copy = pltpu.make_async_copy(src, dst, lsem.at[used[0]])
        used[0] += 1
        copy.start()
        return copy

    def remote(src, dst, peer):
        if len(sent) >= SENDS:
            sent[-SENDS].wait_send()
        copy = pltpu.make_async_remote_copy(
            src_ref=src, dst_ref=dst, send_sem=ssem.at[len(sent) % SENDS], recv_sem=rsem.at[used[1]],
            device_id=peer, device_id_type=MESH,
        )
        used[1] += 1
        used[2] = max(used[2], used[1])
        copy.start()
        sent.append(copy)
        return copy

    msize = ND // MCHUNK
    mom_in = [local(mom.at[pl.ds(i * msize, msize)], mv.at[pl.ds(i * msize, msize)]) for i in range(MCHUNK)]
    for peer in peers:
        pl.semaphore_signal(barrier, inc=1, device_id=peer, device_id_type=MESH)
    used[0] = 12
    dip_in = local(dip_t, dpad.at[pl.ds(mine, RANK)])
    coup_in = local(coup, w_own)
    read_in = local(read_t, rpad.at[pl.ds(mine, RANK)])
    obs_in = local(obs, obsv)
    dpad[pl.ds(other, RANK), :] = jnp.zeros((RANK, ND), BF16)
    rpad[pl.ds(other, RANK), :] = jnp.zeros((RANK, RDEV), BF16)
    members = MEMB // MCHUNK

    for i in range(MCHUNK):
        mom_in[i].wait()
        for r in range(ROWS):
            mbits[i * members:(i + 1) * members, r * 128:(r + 1) * 128] = mv[
                pl.ds(i * msize + r, members, stride=ROWS), :
            ].astype(BF16)
    used[0] = 0
    near_in = [
        local(near.at[pl.ds(i * NROWS, NROWS)], nearv.at[pl.ds(i * NROWS, NROWS)]) for i in range(NCHUNK)
    ]
    dip_in.wait()
    sk[...] = nt(mbits[...], dpad[...])
    pl.semaphore_wait(barrier, len(peers))

    sk_copy = remote(sk.at[pl.ds(other, HALF)], sk_in, sibling)
    first = []
    for step in (2, 1, 3):
        for p in range(3):
            for on, rows, place in ((core, mine, same[p]), (1 - core, other, cross[p])):
                source = sk.at[pl.ds(pl.multiple_of(rows + PART_START[p], 8), PART_ROWS[p])]
                first.append(remote(source, place.at[step - 1], along(PART_AXES[p][0], step, on)))

    coup_in.wait()
    lane = lax.broadcasted_iota(jnp.int32, (RANK, 128), 1)
    row = lax.broadcasted_iota(jnp.int32, (RANK, 128), 0)
    inner = jnp.maximum(row, lane % RANK)

    def split(value):
        upper = value.astype(BF16)
        return upper, (value - upper.astype(F32)).astype(BF16)

    def mask_step(q, _):
        cols = pl.ds(pl.multiple_of(q * 128, 128), 128)
        limit = jnp.where(lane < RANK, ranks[0, 2 * q], ranks[0, 2 * q + 1])
        value = jnp.where(inner < limit, w_own[:, cols], 0.0)
        w_own[:, cols] = value
        upper, rest = split(value)
        wb[pl.ds(mine, RANK), cols] = upper
        wb[pl.ds(128 + mine, RANK), cols] = rest
        return 0

    lax.fori_loop(0, 24, mask_step, 0)

    def near_step(i):
        near_in[i].wait()
        part = nn(mbits[:, i * NROWS:(i + 1) * NROWS], nearv[i * NROWS:(i + 1) * NROWS, :])
        if i == 0:
            mis[...] = part
        else:
            mis[...] += part

    sk_copy.wait_recv()
    block = sk[pl.ds(mine, HALF), :] + sk_in[...]
    for p in range(3):
        ag[p][0, 0, 0] = block[PART_START[p]:PART_START[p] + PART_ROWS[p]]
    for copy in first:
        copy.wait_recv()
    for p in range(3):
        for step in (1, 2, 3):
            ag[p][0, 0, 4 - step] = same[p][step - 1] + cross[p][step - 1]
    second = []
    for step in (2, 1, 3):
        for p in range(3):
            second.append(remote(ag[p].at[0, 0], ag[p].at[0, 4 - step], along(PART_AXES[p][1], step)))
    early = []
    for p in range(3):
        axis = PART_AXES[p][2]
        early.append(remote(ag[p].at[0, 0], ag[p].at[3, 0], along(axis, 1)))
        early.append(remote(ag[p].at[0, 0], ag[p].at[1, 0], along(axis, 3)))
    lax.fori_loop(24, 64, mask_step, 0)
    read_in.wait()
    valid = lax.broadcasted_iota(jnp.int32, (HALF, RDEV), 1) < counts[0, 0]
    read_out[...] = jnp.where(valid, rpad[pl.ds(mine, RANK), :].astype(F32), 0.0)
    read_copy = remote(read_out, read_in_f32, sibling)
    for i in range(0, 2):
        near_step(i)
    for copy in second:
        copy.wait_recv()
    third, relay, rest = [], [], []
    for p in range(3):
        axis = PART_AXES[p][2]
        third.append(remote(ag[p].at[0, 1], ag[p].at[3, 1], along(axis, 1)))
        third.append(remote(ag[p].at[0, 2], ag[p].at[1, 2], along(axis, 3)))
        third.append(remote(ag[p].at[0, 3], ag[p].at[1, 3], along(axis, 3)))
    for p in range(3):
        early[2 * p].wait_recv()
        relay.append(remote(ag[p].at[3, 0], ag[p].at[2, 0], along(PART_AXES[p][2], 1)))
    for p in range(3):
        axis = PART_AXES[p][2]
        rest.append(remote(ag[p].at[0, pl.ds(2, 2)], ag[p].at[3, pl.ds(2, 2)], along(axis, 1)))
        rest.append(remote(ag[p].at[0, 1], ag[p].at[1, 1], along(axis, 3)))
    w_copy = remote(w_own, w_sib, sibling)
    for i in range(2, 5):
        near_step(i)
    for p in range(3):
        axis = PART_AXES[p][2]
        third[3 * p].wait_recv()
        relay.append(remote(ag[p].at[3, 1], ag[p].at[2, 1], along(axis, 1)))
        third[3 * p + 1].wait_recv()
        relay.append(remote(ag[p].at[1, 2], ag[p].at[2, 2], along(axis, 3)))
    for p in range(3):
        third[3 * p + 2].wait_recv()
        relay.append(remote(ag[p].at[1, 3], ag[p].at[2, 3], along(PART_AXES[p][2], 3)))
    w_copy.wait_recv()

    def sibling_step(q, _):
        cols = pl.ds(pl.multiple_of(q * 512, 512), 512)
        upper, rest = split(w_sib[:, cols])
        wb[pl.ds(other, RANK), cols] = upper
        wb[pl.ds(128 + other, RANK), cols] = rest
        return 0

    lax.fori_loop(0, 16, sibling_step, 0)
    for i in range(16):
        wt[i * 512:(i + 1) * 512, :] = wb[:, i * 512:(i + 1) * 512].T
    for i in range(5, NCHUNK):
        near_step(i)
    obs_in.wait()
    mis[...] = mis[...] - obsv[...]
    dif[...] = mis[pl.ds(other, HALF), :]
    dif_copy = remote(dif, dif_in, sibling)
    read_copy.wait_recv()
    rsib[pl.ds(other, RANK), :] = read_in_f32[...].astype(BF16)
    rsib[pl.ds(mine, RANK), :] = jnp.zeros((RANK, RDEV), BF16)
    for p in range(3):
        early[2 * p + 1].wait_recv()
    for copy in rest + relay:
        copy.wait_recv()

    def columns(ax, ay):
        q = (pos[0] + ax) % 4 * 16 + (pos[1] + ay) % 4 * 4
        return pl.ds(pl.multiple_of(q * 128, 512), 512)

    total = None
    for ax in range(4):
        for ay in range(4):
            blocks = []
            for qz in range(4):
                az = (qz + 4 - pos[2]) % 4
                blocks.append(jnp.concatenate([ag0[az, ay, ax], ag1[ax, az, ay], ag2[ay, ax, az]], axis=0))
            upper, rest = split(jnp.concatenate(blocks, axis=1))
            part = nn(jnp.concatenate([upper, rest], axis=0), wt[columns(ax, ay), :])
            total = part if total is None else total + part
    comb[...] = total[:HALF, :128] + (total[:HALF, 128:] + total[HALF:, :128])
    comb_copy = remote(comb, comb_in, sibling)

    def residual(rows, source):
        value = jnp.where(valid, mis[pl.ds(rows, HALF), :] + nn(source[...].astype(BF16), rpad[...]), 0.0)
        mis[pl.ds(rows, HALF), :] = value
        value = value.astype(BF16)
        rb[pl.ds(rows, HALF), :] = value
        return value

    dif_copy.wait_recv()
    here = residual(mine, comb)
    there = (dif_in[...] + nn(comb[...].astype(BF16), rsib[...])).astype(BF16)
    pair = (nt(here, rpad[...]) + nt(there, rsib[...])).astype(BF16)
    pair = jnp.concatenate([pair, pair], axis=1)
    lanes = lax.broadcasted_iota(jnp.int32, (MEMB, 128), 1)

    def edge_cols(array, start, stop, low, high):
        for r in range(start, stop):
            value = array[:, r * 128:(r + 1) * 128].astype(F32)
            turned = pltpu.roll(value, r, 1) if r else value
            low = jnp.where(lanes == r, turned, low)
            high = jnp.where(lanes == (r + 127) % 128, turned, high)
        return low, high

    blank = jnp.zeros((MEMB, 128), F32)

    def grad_step(i):
        grad[:, i * NROWS:(i + 1) * NROWS] = nt(rb[...], nearv[i * NROWS:(i + 1) * NROWS, :])

    def partial_step(ax, ay):
        for half in range(2):
            q = (pos[0] + ax) % 4 * 16 + (pos[1] + ay) % 4 * 4 + 2 * half
            value = nn(pair, wb[:, pl.ds(pl.multiple_of(q * 128, 256), 256)])
            for qz in range(2):
                az = (2 * half + qz + 4 - pos[2]) % 4
                piece = value[:, qz * 128:(qz + 1) * 128]
                rs0[az, ay, ax] = piece[PART_START[0]:PART_START[1]]
                rs1[ax, az, ay] = piece[PART_START[1]:PART_START[2]]
                rs2[ay, ax, az] = piece[PART_START[2]:]

    used[1] = 0
    opp = {}

    def send_opposite(p):
        axis = PART_AXES[p][2]
        opp[p, 1] = remote(rs[p].at[2, 1], rin[p].at[0], along(axis, 1))
        opp[p, 2] = remote(rs[p].at[2, 2], rin[p].at[1], along(axis, 3))
        opp[p, 3] = remote(rs[p].at[2, 3], rin[p].at[2], along(axis, 3))

    for ay in range(4):
        partial_step(2, ay)
    send_opposite(1)
    for ax in (0, 1, 3):
        partial_step(ax, 2)
    send_opposite(2)
    for ax in (0, 1, 3):
        for ay in (0, 1, 3):
            partial_step(ax, ay)
    send_opposite(0)
    direct = []
    for p in (1, 2, 0):
        axis = PART_AXES[p][2]
        direct.append(remote(rs[p].at[1, pl.ds(2, 2)], rin[p].at[pl.ds(4, 2)], along(axis, 1)))
        direct.append(remote(rs[p].at[3, 1], rin[p].at[3], along(axis, 3)))
        opp[p, 0] = remote(rs[p].at[2, 0], rin[p].at[6], along(axis, 1))
    comb_copy.wait_recv()
    residual(other, comb_in)
    used[0] = 0
    outs = [local(mv, mom_out), local(mis, mis_out)]
    grid_row = lat * 16 + lax.broadcasted_iota(jnp.int32, (16, 128), 0)
    spacing = 2.0 * lat_limit / 128
    latitude = -lat_limit + (grid_row.astype(F32) + 0.5) * spacing
    centre = jnp.cos(latitude)
    c_lon = 0.25 / (centre * centre)
    c_north = 0.25 * jnp.cos(latitude + 0.5 * spacing) / centre
    c_south = 0.25 * jnp.cos(latitude - 0.5 * spacing) / centre
    scale = step_size / (1.0 + c_north + c_south + 2.0 * c_lon)
    coef[0] = scale
    coef[1] = jnp.where(grid_row < 127, scale * c_north, 0.0)
    coef[2] = jnp.where(grid_row > 0, scale * c_south, 0.0)
    coef[3] = scale * c_lon
    outs.append(local(coef, coef_out))
    low, high = edge_cols(dpad, 0, ROWS, blank, blank)
    base_w[...] = low.astype(BF16)
    base_e[...] = high.astype(BF16)
    for i in range(0, 2):
        grad_step(i)
    dep, late = [], []
    for p in (1, 2, 0):
        axis = PART_AXES[p][2]
        opp[p, 1].wait_recv()
        rs[p][1, 1] = rs[p][1, 1] + rin[p][0]
        dep.append(remote(rs[p].at[1, 1], rin[p].at[7], along(axis, 1)))
        opp[p, 2].wait_recv()
        rs[p][3, 2] = rs[p][3, 2] + rin[p][1]
        dep.append(remote(rs[p].at[3, 2], rin[p].at[8], along(axis, 3)))
    for p in (1, 2, 0):
        opp[p, 3].wait_recv()
        rs[p][3, 3] = rs[p][3, 3] + rin[p][2]
        dep.append(remote(rs[p].at[3, 3], rin[p].at[9], along(PART_AXES[p][2], 3)))
    for p in (1, 2, 0):
        axis = PART_AXES[p][2]
        late.append(remote(rs[p].at[3, 0], rin[p].at[10], along(axis, 3)))
        opp[p, 0].wait_recv()
        rs[p][1, 0] = rs[p][1, 0] + rin[p][6]
        late.append(remote(rs[p].at[1, 0], rin[p].at[11], along(axis, 1)))
    for i in range(2, 10):
        grad_step(i)
    for copy in direct + dep:
        copy.wait_recv()
    near_owner = []
    for p in range(3):
        rs[p][0, 2] = rs[p][0, 2] + rin[p][4] + rin[p][8]
        near_owner.append(remote(rs[p].at[0, 2], two[p].at[1], along(PART_AXES[p][1], 2)))
    for p in range(3):
        rs[p][0, 1] = rs[p][0, 1] + rin[p][3] + rin[p][7]
        near_owner.append(remote(rs[p].at[0, 1], two[p].at[0], along(PART_AXES[p][1], 1)))
        rs[p][0, 3] = rs[p][0, 3] + rin[p][5] + rin[p][9]
        near_owner.append(remote(rs[p].at[0, 3], two[p].at[2], along(PART_AXES[p][1], 3)))
    for i in range(10, NCHUNK):
        grad_step(i)
    for copy in late:
        copy.wait_recv()
    for p in range(3):
        rs[p][0, 0] = rs[p][0, 0] + rin[p][10] + rin[p][11]
    for copy in near_owner:
        copy.wait_recv()
    last = []
    for p in range(3):
        rs[p][0, 0] = rs[p][0, 0] + two[p][0] + two[p][1] + two[p][2]
    for step in (2, 1, 3):
        for p in range(3):
            for on, place in ((core, one[p]), (1 - core, far_one[p])):
                last.append(remote(rs[p].at[0, 0, step], place.at[step - 1], along(PART_AXES[p][0], step, on)))
    for p in range(3):
        last.append(remote(rs[p].at[0, 0, 0], far_one[p].at[3], sibling))
    low, high = edge_cols(grad, 0, ROWS, blank, blank)
    edge_w[...] = low
    edge_e[...] = high
    for copy in last:
        copy.wait_recv()
    for p in range(3):
        for rows, value in (
            (mine, rs[p][0, 0, 0] + one[p][0] + one[p][1] + one[p][2]),
            (other, far_one[p][0] + far_one[p][1] + far_one[p][2] + far_one[p][3]),
        ):
            own[pl.ds(pl.multiple_of(rows + PART_START[p], 8), PART_ROWS[p]), :] = value
    owner = own[...].astype(BF16)

    def far_grad(start, width):
        cols = pl.ds(start, width)
        grad[:, cols] = grad[:, cols] + nn(owner, dpad[:, cols])

    edge_w[...] = edge_w[...] + nn(owner, base_w[...])
    edge_e[...] = edge_e[...] + nn(owner, base_e[...])
    borders = [remote(edge_w, he, west), remote(edge_e, hw, east)]
    for layer in range(3):
        cols = pl.ds(layer * 128, 128)
        start = layer * 2048
        far_grad(start, 128)
        borders.append(remote(grad.at[:, pl.ds(start, 128)], hn.at[:, cols], south))
        far_grad(start + 15 * 128, 128)
        borders.append(remote(grad.at[:, pl.ds(start + 15 * 128, 128)], hs.at[:, cols], north))
    for layer in range(3):
        for start in range(128, 1920, 256):
            far_grad(layer * 2048 + start, 256)
        cols = pl.ds(layer * 2048, 2048)
        outs.append(local(grad.at[:, cols], grad_out.at[:, cols]))
    for copy in borders:
        copy.wait_recv()
    halo[:, 0:384] = hn[...]
    halo[:, 384:768] = hs[...]
    from_west = pltpu.roll(hw[...], 2, 1)
    halo[:, 768:896] = jnp.where(lanes % 2 == 0, he[...], from_west)
    halo[:, 896:1024] = jnp.where(lanes % 2 == 1, he[...], from_west)
    outs.append(local(halo, halo_out))
    for copy in sent[-SENDS:]:
        copy.wait_send()
    assert used[2] <= RECVS
    for copy in outs:
        copy.wait()


def smooth_kernel(mom, grad, mis, halo, coef, out, mis_out):
    members = mis_out.shape[0]
    mis_out[...] = mis[...]
    lanes = lax.broadcasted_iota(jnp.int32, (members, 128), 1)
    edges = (halo[:, 768:896], halo[:, 896:1024])
    for r in range(ROWS):
        layer, row = r // 16, r % 16
        if row == 0:
            below = halo[:, 384 + layer * 128:384 + (layer + 1) * 128]
            here = grad[:, r * 128:(r + 1) * 128]
        if row == 15:
            above = halo[:, layer * 128:(layer + 1) * 128]
        else:
            above = grad[:, (r + 1) * 128:(r + 2) * 128]
        edge = pltpu.roll(edges[r % 2], 127 - r, 1)
        right = jnp.where(lanes == 127, edge, pltpu.roll(here, 127, 1))
        left = jnp.where(lanes == 0, edge, pltpu.roll(here, 1, 1))
        change = (
            coef[0, row:row + 1, :] * here
            + coef[1, row:row + 1, :] * above
            + coef[2, row:row + 1, :] * below
            + coef[3, row:row + 1, :] * (right + left)
        )
        out[pl.ds(r, members, stride=ROWS), :] = mom[pl.ds(r, members, stride=ROWS), :] - change
        below, here = here, above


def shards(moments, observed, counts, near_kernel, dipole_basis, reading_basis, coupling, ranks):
    mom = moments.reshape(MEMB * ROWS, 128)
    hbm = pl.BlockSpec(memory_space=pl.ANY)
    smem = pl.BlockSpec(memory_space=pltpu.SMEM)
    vmem = pltpu.VMEM
    parts = PART_ROWS
    grad, loaded, misfit, halo, coef = pl.pallas_call(
        exchange_kernel,
        out_shape=[
            vmem((MEMB, ND), F32),
            vmem((MEMB * ROWS, 128), F32),
            vmem((MEMB, RDEV), F32),
            vmem((MEMB, 1024), F32),
            vmem((4, 16, 128), F32),
        ],
        in_specs=[hbm, hbm, smem, hbm, hbm, hbm, hbm, smem],
        out_specs=[hbm] * 5,
        scratch_shapes=[
            vmem((MEMB, ND), F32),
            vmem((MEMB * ROWS, 128), F32),
            vmem((MEMB, RDEV), F32),
            vmem((MEMB, 1024), F32),
            vmem((4, 16, 128), F32),
            vmem((WIDE, 256), BF16),
            vmem((MEMB, ND), BF16),
            vmem((ND, RDEV), BF16),
            vmem((128, ND), BF16),
            vmem((128, RDEV), BF16),
            vmem((MEMB, RDEV), F32),
            vmem((RANK, WIDE), F32),
            vmem((RANK, WIDE), F32),
            vmem((256, WIDE), BF16),
            vmem((MEMB, RDEV), BF16),
            vmem((MEMB, 128), F32),
            vmem((HALF, 128), F32),
            vmem((HALF, 128), F32),
            vmem((HALF, 128), F32),
            vmem((RANK, RDEV), F32),
            vmem((RANK, RDEV), F32),
            vmem((128, RDEV), BF16),
            vmem((HALF, RDEV), F32),
            vmem((HALF, RDEV), F32),
            vmem((MEMB, 128), F32),
            vmem((MEMB, 128), F32),
            vmem((MEMB, 128), F32),
            vmem((128, 128), BF16),
            vmem((128, 128), BF16),
            vmem((MEMB, 384), F32),
            vmem((MEMB, 384), F32),
            vmem((MEMB, 128), F32),
            vmem((MEMB, 128), F32),
        ]
        + [vmem((4, 4, 4, n, 128), F32) for n in parts]
        + [vmem((4, 4, 4, n, 128), F32) for n in parts]
        + [vmem((12, 4, n, 128), F32) for n in parts]
        + [vmem((3, 4, n, 128), F32) for n in parts]
        + [vmem((3, n, 128), F32) for n in parts]
        + [vmem((4, n, 128), F32) for n in parts]
        + [vmem((3, n, 128), F32) for n in parts] * 2
        + [pltpu.SemaphoreType.DMA((SENDS,)), pltpu.SemaphoreType.DMA((RECVS,)), pltpu.SemaphoreType.DMA((16,))],
        compiler_params=pltpu.CompilerParams(
            collective_id=0, has_side_effects=True, vmem_limit_bytes=48 * 1024 * 1024
        ),
        cost_estimate=pl.CostEstimate(flops=3_700_000_000, bytes_accessed=24_000_000, transcendentals=0),
        name="exchange",
    )(
        mom, observed[0, 0], counts, near_kernel[0, 0], dipole_basis[0, 0].T, reading_basis[0, 0].T,
        coupling[0, 0], ranks[0],
    )
    members = 32
    new, misfit = pl.pallas_call(
        smooth_kernel,
        grid=(MEMB // members,),
        out_shape=[
            jax.ShapeDtypeStruct((MEMB * ROWS, 128), F32),
            jax.ShapeDtypeStruct((MEMB, RDEV), F32),
        ],
        in_specs=[
            pl.BlockSpec((members * ROWS, 128), lambda i: (i, 0)),
            pl.BlockSpec((members, ND), lambda i: (i, 0)),
            pl.BlockSpec((members, RDEV), lambda i: (i, 0)),
            pl.BlockSpec((members, 1024), lambda i: (i, 0)),
            pl.BlockSpec((4, 16, 128), lambda i: (0, 0, 0)),
        ],
        out_specs=[
            pl.BlockSpec((members * ROWS, 128), lambda i: (i, 0)),
            pl.BlockSpec((members, RDEV), lambda i: (i, 0)),
        ],
        compiler_params=pltpu.CompilerParams(vmem_limit_bytes=32 * 1024 * 1024),
        cost_estimate=pl.CostEstimate(flops=10_000_000, bytes_accessed=4_000_000, transcendentals=0),
        name="smooth",
    )(loaded, grad, misfit, halo, coef)
    return new.reshape(moments.shape), misfit[None, None]


def solution(mesh):
    return jax.shard_map(
        shards,
        mesh=mesh,
        in_specs=(
            P(None, None, "lat", "lon"),
            P("lat", "lon", None, None),
            P("lat", "lon"),
            P("lat", "lon", None, None),
            P("lat", "lon", None, None),
            P("lat", "lon", None, None),
            P("lat", "lon", None, None),
            P("lat", "lon", None),
        ),
        out_specs=(P(None, None, "lat", "lon"), P("lat", "lon", None, None)),
        check_vma=False,
    )
```
